256 devices in a mesh: ctx: 32 (over z, x_lo, core), tp: 8 (over x_hi, y).
Axes of the slice: x: 4 (x_hi: 2, x_lo: 2; x = x_hi * 2 + x_lo), y: 4, z: 8, core: 2. Of those that a mesh axis runs over, the one named last changes fastest.
Arguments:
- layer_input: bfloat16 [16384, 5376], P('ctx', 'tp'), may hold values from -60 to 60
- norm_weight: bfloat16 [5376], P('tp'), may hold values from 0.099609375 to 1.8984375
- document_index: int32 [16384], P('ctx'), may hold values from 0 to 7, never falling along the last dimension, each value on 1 to 8192 neighbouring positions
- stored_queries: bfloat16 [16384, 4096], P('ctx', 'tp'), may hold values from -6 to 6
- stored_keys: bfloat16 [16384, 2048], P('ctx', 'tp'), may hold values from -6 to 6
- stored_values: bfloat16 [16384, 2048], P('ctx', 'tp'), may hold values from -6 to 6
- output_weight: bfloat16 [4096, 5376], P(None, 'tp'), may hold values from -0.1500248 to 0.1500248
- projection_gradient: bfloat16 [16384, 5376], P('ctx', 'tp'), may hold values from -600 to 600
- adapter_down_maps: bfloat16 [5376, 24], P('tp'), may hold values from -0.078125 to 0.078125
Outputs:
- feature_q: float32 [8, 4096], P(None, 'tp')
- feature_k: float32 [8, 2048], P(None, 'tp')
- feature_v: float32 [8, 2048], P(None, 'tp')
The draws below stay inside these ranges and needn't reach their ends.
Inputs may be any that keep to these rules, and one draw needn't show every extreme that they name: `document_index`: document numbers never fall along the sequence; every document is one run of positions.
All inputs are finite; a program needn't handle non-finite values.
Results may differ from the reference program's by a relative error of at most 0.0095.
Values may be sent and summed in bfloat16 or wider, within the bound.
A program may use at most 128 MiB of HBM per device.

```python
import math
import jax
import jax.numpy as jnp
import numpy as np
from jax import lax

MODEL_WIDTH = 5376
QUERY_HEADS = 32
KEY_VALUE_HEADS = 16
HEAD_SIZE = 128
LOOKBACK_SPAN = 1024
ADAPTER_RANK = 8
TOK_DEV = 512
SEQUENCE_TOKENS = 16384
DOCS = 8


def paired_states(key):
    base = jax.random.fold_in(key, 11)
    key_query, key_random_seeds = jax.random.split(base, 2)
    query_draw = jax.random.normal(key_query, (SEQUENCE_TOKENS, QUERY_HEADS * HEAD_SIZE), jnp.float32)
    key_sample = jax.random.normal(key_random_seeds, (SEQUENCE_TOKENS, KEY_VALUE_HEADS * HEAD_SIZE), jnp.float32)
    return (jnp.clip(query_draw, -6.0, 6.0), jnp.clip(key_sample, -6.0, 6.0))


def draw_stored_queries(key, part):
    return paired_states(key)[0].astype(jnp.bfloat16)


def draw_stored_keys(key, part):
    return paired_states(key)[1].astype(jnp.bfloat16)


def draw_layer_input(key, part):
    key_main, key_cols = jax.random.split(jax.random.fold_in(key, 31), 2)
    col_scale = jnp.exp(jax.random.uniform(key_cols, (1, MODEL_WIDTH), jnp.float32, 0.0, math.log(10.0)))
    values = jax.random.normal(key_main, (SEQUENCE_TOKENS, MODEL_WIDTH), jnp.float32)
    return (jnp.clip(values, -6.0, 6.0) * col_scale).astype(jnp.bfloat16)


def draw_projection_gradient(key, part):
    key_main, key_rows, key_cols = jax.random.split(jax.random.fold_in(key, 23), 3)
    along = jnp.arange(SEQUENCE_TOKENS, dtype=jnp.float32) / max(SEQUENCE_TOKENS - 1, 1)
    row_scale = jnp.exp(jax.random.uniform(key_rows, (SEQUENCE_TOKENS, 1), jnp.float32, 0.0, math.log(10.0)))
    col_scale = jnp.exp(jax.random.uniform(key_cols, (1, MODEL_WIDTH), jnp.float32, 0.0, math.log(10.0)))
    rising = jnp.exp(math.log(3.0) * along)[:, None]
    values = jax.random.normal(key_main, (SEQUENCE_TOKENS, MODEL_WIDTH), jnp.float32)
    return (jnp.clip(values, -6.0, 6.0) * rising * row_scale * col_scale / 10.0).astype(jnp.bfloat16)


def draw_output_weight(key, part):
    key_main = jax.random.fold_in(key, 41)
    along = jnp.arange(QUERY_HEADS * HEAD_SIZE, dtype=jnp.float32) / (QUERY_HEADS * HEAD_SIZE - 1) - 0.5
    rising = jnp.exp(math.log(3.0) * along)[:, None]
    values = jax.random.normal(key_main, (QUERY_HEADS * HEAD_SIZE, MODEL_WIDTH), jnp.float32)
    return (jnp.clip(values, -6.0, 6.0) * rising * float(MODEL_WIDTH) ** (-0.5)).astype(jnp.bfloat16)


def levels(own_key, extent, cuts, low, top_value):
    loudness, own = 1.0, jax.random.fold_in(own_key, 6)
    for axis_at, shards_of in cuts:
        draws = jnp.exp(jax.random.uniform(jax.random.fold_in(own, axis_at), (shards_of,), jnp.float32, low / len(cuts), top_value / len(cuts)))
        loudness = loudness * jnp.repeat(draws, extent[axis_at] // shards_of).reshape([-1 if axis == axis_at else 1 for axis in range(len(extent))])
    return loudness


def profile(number_of, total, reach, lean):
    weights = [(1 << 20) // math.isqrt(standing ** lean) + 1 for standing in range(2, number_of + 1)]
    surplus, given = total - reach - (number_of - 1), [1] * (number_of - 1)
    while surplus > 0:
        movable = [i for i in range(number_of - 1) if given[i] < reach]
        pool, remaining = sum([weights[i] for i in movable]), surplus
        for i in movable:
            extra = min(reach - given[i], max(1, remaining * weights[i] // pool), surplus)
            given[i] = given[i] + extra
            surplus = surplus - extra
    return np.array([reach] + given)


def uneven_parts(own_key, amount, total, bound, skew):
    if amount == 2:
        one = jax.random.randint(own_key, (), max(1, total - bound), min(bound, total - 1) + 1)
        return jnp.stack([one, total - one])
    sizes = jnp.asarray(profile(amount, total, bound, skew), jnp.int32)
    pairs = (amount - 1) // 2
    source_of, receiver = sizes[1:1 + 2 * pairs:2], sizes[2:2 + 2 * pairs:2]
    slack = jnp.minimum(source_of - 1, bound - receiver)
    moved = jax.random.randint(jax.random.fold_in(own_key, 1), (pairs,), 0, 1 << 20) % (slack + 1)
    sizes = sizes.at[1:1 + 2 * pairs:2].set(source_of - moved).at[2:2 + 2 * pairs:2].set(receiver + moved)
    return sizes[jax.random.permutation(jax.random.fold_in(own_key, 2), amount)]


def scatter_about(own_key, shape, spread, bound, cuts=(), kind=jnp.bfloat16):
    drawn = spread * jax.random.normal(own_key, shape, jnp.float32)
    if cuts:
        drawn = drawn * levels(own_key, shape, cuts, -0.22, 0.18)
    return jnp.clip(drawn, -bound, bound).astype(kind)


def setup_inputs(seed: int = 0) -> dict:
    splits = jax.random.split(jax.random.key(seed), 10)
    return {
        "layer_input": draw_layer_input(jax.random.fold_in(splits[9], 71), 0),
        "norm_weight": jnp.clip(1.0 + 0.18 * jax.random.normal(splits[1], (MODEL_WIDTH,), jnp.float32), 0.099609375, 1.8984375).astype(jnp.bfloat16),
        "document_index": jnp.searchsorted(jnp.cumsum(uneven_parts(splits[2], DOCS, SEQUENCE_TOKENS, SEQUENCE_TOKENS // 2, 2)), jnp.arange(SEQUENCE_TOKENS), side="right").astype(jnp.int32),
        "stored_queries": draw_stored_queries(jax.random.fold_in(splits[9], 71), 0),
        "stored_keys": draw_stored_keys(jax.random.fold_in(splits[9], 71), 0),
        "stored_values": scatter_about(splits[5], (SEQUENCE_TOKENS, KEY_VALUE_HEADS * HEAD_SIZE), 1.0, 6.0, ((0, 32), (1, 8))),
        "output_weight": draw_output_weight(jax.random.fold_in(splits[9], 71), 0),
        "projection_gradient": draw_projection_gradient(jax.random.fold_in(splits[9], 71), 0),
        "adapter_down_maps": scatter_about(splits[8], (MODEL_WIDTH, 3 * ADAPTER_RANK), MODEL_WIDTH ** -0.5, 0.078125, ((0, 8),)),
    }


def attend_block(query_block, key_block, value_block, gradient_block, allowed, softmax_scale):
    query_wide = query_block.astype(jnp.float32)
    key_wide = key_block.astype(jnp.float32)
    value_wide = value_block.astype(jnp.float32)
    grad_wide = gradient_block.astype(jnp.float32)
    scores = jnp.einsum('sgrd,kgd->grsk', query_wide, key_wide) * softmax_scale
    scores = jnp.where(allowed[None, None], scores, -1e+30)
    highest = lax.optimization_barrier(jnp.max(scores, axis=-1, keepdims=True))
    expons = jnp.exp(scores - highest)
    probs = expons / lax.optimization_barrier(jnp.sum(expons, axis=-1, keepdims=True))
    probs_low = probs.astype(jnp.bfloat16).astype(jnp.float32)
    attended = jnp.einsum('grsk,kgd->sgrd', probs_low, value_wide)
    delta = jnp.einsum('sgrd,sgrd->grs', grad_wide, attended)
    grad_probs = jnp.einsum('sgrd,kgd->grsk', grad_wide, value_wide)
    grad_scores = (probs * (grad_probs - delta[..., None]) * softmax_scale).astype(jnp.bfloat16).astype(jnp.float32)
    query_gradient = jnp.einsum('grsk,kgd->sgrd', grad_scores, key_wide)
    key_gradient = jnp.einsum('grsk,sgrd->kgd', grad_scores, query_wide)
    value_gradient = jnp.einsum('grsk,sgrd->kgd', probs_low, grad_wide)
    return (query_gradient, key_gradient, value_gradient)

def reference(layer_input, norm_weight, document_index, stored_queries, stored_keys, stored_values, output_weight, projection_gradient, adapter_down_maps):
    hidden_wide = layer_input.astype(jnp.float32)
    normalized_input = (hidden_wide * lax.rsqrt(lax.optimization_barrier(jnp.mean(hidden_wide * hidden_wide, axis=-1, keepdims=True)) + 1e-06) * norm_weight.astype(jnp.float32)).astype(jnp.bfloat16)
    reduced_rank = jnp.dot(normalized_input, adapter_down_maps, preferred_element_type=jnp.float32).astype(jnp.bfloat16)
    output_gradient = jnp.dot(projection_gradient, output_weight.T, preferred_element_type=jnp.float32).astype(jnp.bfloat16)
    overall_rows = stored_queries.shape[0]
    query_groups = QUERY_HEADS // KEY_VALUE_HEADS
    rows_per_block = TOK_DEV
    window_rows = rows_per_block + LOOKBACK_SPAN
    key_padded = jnp.concatenate([jnp.zeros((LOOKBACK_SPAN, KEY_VALUE_HEADS * HEAD_SIZE), stored_keys.dtype), stored_keys], 0)
    value_padded = jnp.concatenate([jnp.zeros((LOOKBACK_SPAN, KEY_VALUE_HEADS * HEAD_SIZE), stored_values.dtype), stored_values], 0)
    id_pad = jnp.concatenate([jnp.full((LOOKBACK_SPAN,), -1, jnp.int32), document_index.astype(jnp.int32)], 0)
    softmax_scale = float(MODEL_WIDTH // QUERY_HEADS) ** (-0.5)

    def one_block(carry, block_index):
        key_gradient_total, value_gradient_total = carry
        start_offset = (block_index * rows_per_block).astype(jnp.int32)
        query_block = lax.dynamic_slice_in_dim(stored_queries, start_offset, rows_per_block, 0).reshape(rows_per_block, KEY_VALUE_HEADS, query_groups, HEAD_SIZE)
        gradient_block = lax.dynamic_slice_in_dim(output_gradient, start_offset, rows_per_block, 0).reshape(rows_per_block, KEY_VALUE_HEADS, query_groups, HEAD_SIZE)
        key_block = lax.dynamic_slice_in_dim(key_padded, start_offset, window_rows, 0).reshape(window_rows, KEY_VALUE_HEADS, HEAD_SIZE)
        value_block = lax.dynamic_slice_in_dim(value_padded, start_offset, window_rows, 0).reshape(window_rows, KEY_VALUE_HEADS, HEAD_SIZE)
        query_ids = lax.dynamic_slice_in_dim(document_index.astype(jnp.int32), start_offset, rows_per_block, 0)
        key_ids = lax.dynamic_slice_in_dim(id_pad, start_offset, window_rows, 0)
        query_pos = start_offset + jnp.arange(rows_per_block, dtype=jnp.int32)
        key_pos = start_offset - LOOKBACK_SPAN + jnp.arange(window_rows, dtype=jnp.int32)
        spacing = query_pos[:, None] - key_pos[None, :]
        allowed = (spacing >= 0) & (spacing < LOOKBACK_SPAN) & (query_ids[:, None] == key_ids[None, :])
        query_gradient, key_gradient, value_gradient = attend_block(query_block, key_block, value_block, gradient_block, allowed, softmax_scale)
        key_previous = lax.dynamic_slice_in_dim(key_gradient_total, start_offset, window_rows, 0)
        key_gradient_total = lax.dynamic_update_slice_in_dim(key_gradient_total, key_previous + key_gradient.reshape(window_rows, KEY_VALUE_HEADS * HEAD_SIZE), start_offset, 0)
        value_previous = lax.dynamic_slice_in_dim(value_gradient_total, start_offset, window_rows, 0)
        value_gradient_total = lax.dynamic_update_slice_in_dim(value_gradient_total, value_previous + value_gradient.reshape(window_rows, KEY_VALUE_HEADS * HEAD_SIZE), start_offset, 0)
        return ((key_gradient_total, value_gradient_total), query_gradient.reshape(rows_per_block, QUERY_HEADS * HEAD_SIZE).astype(jnp.bfloat16))
    blank_block = jnp.zeros((overall_rows + LOOKBACK_SPAN, KEY_VALUE_HEADS * HEAD_SIZE), jnp.float32)
    (key_gradient_total, value_gradient_total), query_grads = lax.scan(one_block, (blank_block, blank_block), jnp.arange(overall_rows // rows_per_block, dtype=jnp.int32))
    query_gradient = query_grads.reshape(overall_rows, QUERY_HEADS * HEAD_SIZE)
    key_gradient = key_gradient_total[LOOKBACK_SPAN:].astype(jnp.bfloat16)
    value_gradient = value_gradient_total[LOOKBACK_SPAN:].astype(jnp.bfloat16)
    adapter_query = jnp.dot(reduced_rank[:, 0:ADAPTER_RANK].T, query_gradient, preferred_element_type=jnp.float32)
    adapter_key = jnp.dot(reduced_rank[:, ADAPTER_RANK:2 * ADAPTER_RANK].T, key_gradient, preferred_element_type=jnp.float32)
    adapter_value = jnp.dot(reduced_rank[:, 2 * ADAPTER_RANK:3 * ADAPTER_RANK].T, value_gradient, preferred_element_type=jnp.float32)
    grand_total = jnp.sum(adapter_query * adapter_query) + jnp.sum(adapter_key * adapter_key) + jnp.sum(adapter_value * adapter_value)
    scale_factor = jnp.sqrt(float(ADAPTER_RANK * (QUERY_HEADS + 2 * KEY_VALUE_HEADS) * HEAD_SIZE) / (grand_total + 1e-06))
    return (adapter_query * scale_factor, adapter_key * scale_factor, adapter_value * scale_factor)
```

```python
import jax
import jax.numpy as jnp
from jax import lax
from jax.experimental import pallas as pl
from jax.experimental.pallas import tpu as pltpu
from jax.sharding import PartitionSpec as P

MODEL_WIDTH = 5376
QUERY_HEADS = 32
KEY_VALUE_HEADS = 16
HEAD_SIZE = 128
LOOKBACK_SPAN = 1024
RANK = 8

CTX = 32
ROWS = 512
WIDTH = 672
QCOLS = 512
KCOLS = 256
WINDOW = 1536
QB = 256
KSPAN = 1280
RC = 128
NRC = ROWS // RC
SCALE = float(MODEL_WIDTH // QUERY_HEADS) ** (-0.5)
LOG2E = 1.4426950408889634

MESH = pl.DeviceIdType.MESH
NT = (((1,), (1,)), ((), ()))
NN = (((1,), (0,)), ((), ()))
F32 = jnp.float32
BF16 = jnp.bfloat16


def dot(a, b, dims=NN):
    return lax.dot_general(a, b, dims, preferred_element_type=F32)


def loop(count, body):
    def step(i, carry):
        body(i)
        return carry

    lax.fori_loop(0, count, step, 0)


def kernel(
    x_ref, nw_ref, doc_ref, q_ref, k_ref, v_ref, w_ref, pg_ref, a_ref,
    oq_ref, ok_ref, ov_ref,
    xs, nws, ids, qs, kx, vx, ws, pgs, am,
    psend, pacc, precv, asend, arecv, xsend, xrecv,
    tmine, trecv, tx_send, tx_recv, lown, lx,
    bias, probs, rv, g, acc, ar, red, fin, sq, sqr,
    load_sem, wload_sem, halo_send, halo_recv,
    p_send, p_recv, a_send, a_recv, x_send, x_recv,
    t1_send, t1_recv, t2_send, t2_recv, t3_send, t3_recv, t4_send, t4_recv,
    ar_send, ar_recv, fin_send, fin_recv, sq_send, sq_recv,
):
    c = lax.axis_index("ctx")
    t = lax.axis_index("tp")
    xh = t // 4
    y = t % 4
    z = c // 4
    low = c % 4
    up = xh * 4 + (y + 1) % 4
    down = xh * 4 + (y + 3) % 4
    across = (t + 4) % 8

    def remote(src, dst, ssem, rsem, cc, tt):
        return pltpu.make_async_remote_copy(
            src_ref=src, dst_ref=dst, send_sem=ssem, recv_sem=rsem,
            device_id=(cc, tt), device_id_type=MESH,
        )

    loads = [
        pltpu.make_async_copy(src, dst, load_sem.at[n])
        for n, (src, dst) in enumerate([
            (x_ref, xs), (nw_ref, nws), (a_ref, am), (pg_ref, pgs), (q_ref, qs),
            (k_ref, kx.at[pl.ds(1024, ROWS), :]), (v_ref, vx.at[pl.ds(1024, ROWS), :]),
            (doc_ref, ids.at[:, pl.ds(1024, ROWS)]),
        ])
    ]
    for copy in loads:
        copy.start()

    def order_of(s):
        first_x = ((s + 1) // 2) % 2
        first_y = 2 + (s // 2) * ((s % 2) * 2 - 1)
        late = s - 4
        late_x = s % 2
        late_y = (1 - late // 2) * (1 + 2 * (s % 2))
        is_late = s // 4
        dx = first_x * (1 - is_late) + late_x * is_late
        dy = first_y * (1 - is_late) + late_y * is_late
        return dx * 4 + (y + dy) % 4

    def wload(s):
        rows = pl.ds(pl.multiple_of(order_of(s) * QCOLS, QCOLS), QCOLS)
        return pltpu.make_async_copy(w_ref.at[rows, :], ws.at[s], wload_sem.at[s])

    loop(8, lambda s: wload(s).start())

    barrier = pltpu.get_barrier_semaphore()

    def greet_ctx(i):
        pl.semaphore_signal(barrier, inc=1, device_id=((c + 1 + i) % CTX, t), device_id_type=MESH)

    def greet_tp(i):
        pl.semaphore_signal(barrier, inc=1, device_id=(c, (t + 1 + i) % 8), device_id_type=MESH)

    loop(CTX - 1, greet_ctx)
    loop(7, greet_tp)

    for copy in loads[:3]:
        copy.wait()
    sel_row = lax.broadcasted_iota(jnp.int32, (32, 3 * RANK), 0)
    sel_col = lax.broadcasted_iota(jnp.int32, (32, 3 * RANK), 1)
    wanted = jnp.where(sel_row < 16, sel_row + 8, jnp.where(sel_row < 24, sel_row - 16, -1))
    select = (wanted == sel_col).astype(BF16)
    maps_t = dot(select, am[...], NT).astype(BF16)
    x_wide = xs[...].astype(F32)
    xw = (x_wide * nws[...].astype(F32)).astype(BF16)
    part = dot(maps_t, xw, NT)
    square = x_wide * x_wide
    square_hi = square.astype(BF16)
    square_lo = (square - square_hi.astype(F32)).astype(BF16)
    ones = jnp.ones((RANK, WIDTH), BF16)
    squares = dot(ones, square_hi, NT) + dot(ones, square_lo, NT)
    for n in range(4):
        cols = slice(n * 128, (n + 1) * 128)
        tmine[n, 0:24, :] = part[0:24, cols]
        tmine[n, 24:32, :] = squares[:, cols]

    pl.semaphore_wait(barrier, CTX - 1 + 7)

    def t1_copy(d):
        dest = (y + d) % 4
        return remote(tmine.at[dest], trecv.at[y], t1_send.at[d], t1_recv.at[y], c, xh * 4 + dest)

    def t1_wait(d):
        src = (y + d) % 4
        remote(tmine.at[y], trecv.at[src], t1_send.at[d], t1_recv.at[src], c, t).wait_recv()
        t1_copy(d).wait_send()

    loop(3, lambda d: t1_copy(d + 1).start())

    def halo_copies(n):
        d = n + 1
        dest = (c + d) % CTX
        rows = pl.ds((2 - d) * ROWS, ROWS)
        return [
            remote(k_ref, kx.at[rows, :], halo_send.at[n, 0], halo_recv.at[n, 0], dest, t),
            remote(doc_ref, ids.at[:, rows], halo_send.at[n, 1], halo_recv.at[n, 1], dest, t),
            remote(v_ref, vx.at[rows, :], halo_send.at[n, 2], halo_recv.at[n, 2], dest, t),
        ]

    halos = [halo_copies(0), halo_copies(1)]
    for m in range(3):
        for n in range(2):
            halos[n][m].start()

    loads[3].wait()

    def rows_of(rc):
        return pl.ds(pl.multiple_of(rc * RC, RC), RC)

    def p_copy(s, rc):
        turn = (y + 1 + 2 * (s % 2)) % 4
        return remote(
            psend.at[s, rows_of(rc), :], precv.at[s, rows_of(rc), :],
            p_send.at[s, rc], p_recv.at[s, rc], c, xh * 4 + turn,
        )

    def early(s):
        wload(s).wait()
        psend[s] = dot(pgs[...], ws[s], NT).astype(BF16)
        loop(NRC, lambda rc: p_copy(s, rc).start())

    loop(4, early)

    loop(3, lambda d: t1_wait(d + 1))
    tsum = tmine[y]
    for d in range(1, 4):
        tsum = tsum + trecv[(y + d) % 4]
    tx_send[...] = tsum
    t2 = remote(tx_send, tx_recv, t2_send, t2_recv, c, across)
    t2.start()

    def late(s):
        wload(s + 4).wait()
        pacc[s] = dot(pgs[...], ws[s + 4], NT)

    loop(4, late)

    t2.wait()
    tfull = tx_send[...] + tx_recv[...]
    rstd = lax.rsqrt(tfull[24:32, :] * (1.0 / MODEL_WIDTH) + 1e-06)
    lown[...] = (tfull * jnp.concatenate([rstd] * 4, axis=0)).astype(BF16)

    def own_cols(n):
        return pl.ds(pl.multiple_of(1024 + n * 128, 128), 128)

    lx[:, own_cols(y)] = lown[...]

    def t3_copy(d):
        return remote(
            lown, lx.at[:, own_cols(y)], t3_send.at[d], t3_recv.at[y], c, xh * 4 + (y + d) % 4
        )

    def t3_wait(d):
        src = (y + d) % 4
        remote(lown, lx.at[:, own_cols(src)], t3_send.at[d], t3_recv.at[src], c, t).wait_recv()
        t3_copy(d).wait_send()

    loop(3, lambda d: t3_copy(d + 1).start())

    def a_copy(s, rc):
        turn = (y + 1 + 2 * s) % 4
        return remote(
            asend.at[s, rows_of(rc), :], arecv.at[s, rows_of(rc), :],
            a_send.at[s, rc], a_recv.at[s, rc], c, xh * 4 + turn,
        )

    def pass_on(i):
        rc, s = i // 2, i % 2
        p_copy(s, rc).wait_recv()
        asend[s, rows_of(rc), :] = (
            pacc[s, rows_of(rc), :] + precv[s, rows_of(rc), :].astype(F32)
        ).astype(BF16)
        a_copy(s, rc).start()

    loop(2 * NRC, pass_on)

    loop(3, lambda d: t3_wait(d + 1))
    t4s = [
        remote(
            lx.at[pl.ds(0, 16), pl.ds(1024, ROWS)], lx.at[pl.ds(0, 16), pl.ds((1 - n) * ROWS, ROWS)],
            t4_send.at[n], t4_recv.at[n], (c + n + 1) % CTX, t,
        )
        for n in range(2)
    ]
    for copy in t4s:
        copy.start()

    for copy in loads[4:]:
        copy.wait()
    for n in range(2):
        halos[n][0].wait()
        halos[n][1].wait()
    key_at = lax.broadcasted_iota(jnp.int32, (1, WINDOW), 1) + c * ROWS - LOOKBACK_SPAN
    key_ids = jnp.where(key_at < 0, -1, ids[...]).astype(F32)
    own_ids = jnp.broadcast_to(key_ids[:, 1024:1536], (128, ROWS))
    query_ids = jnp.transpose(own_ids, (1, 0))
    row_at = lax.broadcasted_iota(jnp.int32, (QB, 128), 0)
    col_at = lax.broadcasted_iota(jnp.int32, (QB, 128), 1)
    for b in range(2):
        for m in range(KSPAN // 128):
            spacing = 1024 - m * 128 + row_at - col_at
            start = b * QB + m * 128
            allowed = (
                (spacing >= 0)
                & (spacing < LOOKBACK_SPAN)
                & (query_ids[b * QB:(b + 1) * QB, :] == key_ids[:, start:start + 128])
            )
            bias[b, :, m * 128:(m + 1) * 128] = jnp.where(allowed, 0.0, -1e30)

    def parts_of(i):
        h, b = i // 2, i % 2
        q_rows = pl.ds(pl.multiple_of(b * QB, QB), QB)
        k_rows = pl.ds(pl.multiple_of(b * QB, QB), KSPAN)
        h_cols = pl.ds(pl.multiple_of(h * HEAD_SIZE, HEAD_SIZE), HEAD_SIZE)
        g_cols = pl.ds(pl.multiple_of((h // 2) * HEAD_SIZE, HEAD_SIZE), HEAD_SIZE)
        return h, b, q_rows, k_rows, h_cols, g_cols

    def softmax(i):
        h, b, q_rows, k_rows, h_cols, g_cols = parts_of(i)
        scores = dot(qs[q_rows, h_cols], kx[k_rows, g_cols], NT) * (SCALE * LOG2E) + bias[b]
        highest = jnp.max(scores, axis=-1, keepdims=True)
        expons = jnp.exp2(scores - highest)
        total = jnp.sum(expons, axis=-1, keepdims=True)
        probs[i] = expons * (1.0 / total)

    loop(8, softmax)

    for copy in t4s:
        copy.wait()

    def value_side(i):
        b = i % 2
        lows = lx[0:16, pl.ds(pl.multiple_of(b * QB, QB), KSPAN)]
        rv[i] = dot(lows, probs[i].astype(BF16), NT)

    loop(8, value_side)

    def x_copy(rc):
        return remote(
            xsend.at[rows_of(rc), :], xrecv.at[rows_of(rc), :],
            x_send.at[rc], x_recv.at[rc], c, across,
        )

    def finish(rc):
        rows = rows_of(rc)
        p_copy(2, rc).wait_recv()
        p_copy(3, rc).wait_recv()
        a_copy(0, rc).wait_recv()
        a_copy(1, rc).wait_recv()
        xsend[rows, :] = (
            pacc[3 - xh, rows, :] + arecv[1 - xh, rows, :].astype(F32)
            + precv[2 + xh, rows, :].astype(F32)
        ).astype(BF16)
        x_copy(rc).start()
        pacc[2 + xh, rows, :] = (
            pacc[2 + xh, rows, :] + arecv[xh, rows, :].astype(F32)
            + precv[3 - xh, rows, :].astype(F32)
        )

    loop(NRC, finish)

    for n in range(2):
        halos[n][2].wait()
    acc[...] = jnp.zeros_like(acc)

    def take(rc):
        rows = rows_of(rc)
        x_copy(rc).wait_recv()
        g[rows, :] = (pacc[2 + xh, rows, :] + xrecv[rows, :].astype(F32)).astype(BF16)

    def backward(b, h):
        i = h * 2 + b
        h, b, q_rows, k_rows, h_cols, g_cols = parts_of(i)
        grad = g[q_rows, h_cols]
        keys = kx[k_rows, g_cols]
        grad_probs = dot(grad, vx[k_rows, g_cols], NT)
        prob = probs[i]
        delta = jnp.sum(prob * grad_probs, axis=-1, keepdims=True)
        grad_scores = (prob * (grad_probs - delta)).astype(BF16)
        lows = lx[0:16, k_rows]
        side_k = (dot(lows, grad_scores, NT) * SCALE).astype(BF16)
        own = lx[16:32, pl.ds(pl.multiple_of(1024 + b * QB, QB), QB)]
        side_q = (dot(own, grad_scores) * SCALE).astype(BF16)
        acc[h] += dot(side_q, keys)[0:8]
        acc[4 + h // 2] += dot(side_k, qs[q_rows, h_cols])[0:8]
        acc[6 + h // 2] += dot(rv[i].astype(BF16), grad)[8:16]

    def block(b):
        loop(2, lambda n: take(b * 2 + n))
        loop(4, lambda h: backward(b, h))

    loop(2, block)

    def ar_copy(d):
        dest = (c + d) % CTX
        return remote(acc.at[dest // 4], ar.at[c], ar_send.at[d], ar_recv.at[c], dest, t)

    def ar_wait(d):
        src = (c + d) % CTX
        remote(acc.at[z], ar.at[src], ar_send.at[d], ar_recv.at[src], c, t).wait_recv()

    loop(CTX - 1, lambda d: ar_copy(d + 1).start())
    ar[c] = acc[z]
    loop(CTX - 1, lambda d: ar_wait(d + 1))
    red[...] = jnp.sum(ar[...], axis=0)

    def fin_copy(d):
        return remote(
            red, fin.at[z], fin_send.at[d], fin_recv.at[z], ((z + d) % 8) * 4 + low, t
        )

    def fin_wait(d):
        src = (z + d) % 8
        remote(red, fin.at[src], fin_send.at[d], fin_recv.at[src], c, t).wait_recv()

    loop(7, lambda d: fin_copy(d + 1).start())
    fin[z] = red[...]
    loop(7, lambda d: fin_wait(d + 1))

    whole = fin[...]
    sq[...] = jnp.sum(whole * whole, axis=0)

    def sq_copy(d):
        return remote(sq, sqr.at[t], sq_send.at[d], sq_recv.at[t], c, (t + d) % 8)

    def sq_wait(d):
        src = (t + d) % 8
        remote(sq, sqr.at[src], sq_send.at[d], sq_recv.at[src], c, t).wait_recv()

    loop(7, lambda d: sq_copy(d + 1).start())
    sqr[t] = sq[...]
    loop(7, lambda d: sq_wait(d + 1))
    squared = jnp.sum(jnp.sum(jnp.sum(sqr[...], axis=0), axis=0, keepdims=True), axis=1, keepdims=True)
    factor = jnp.sqrt(
        float(RANK * (QUERY_HEADS + 2 * KEY_VALUE_HEADS) * HEAD_SIZE) / (squared + 1e-06)
    )
    for n in range(4):
        oq_ref[:, n * 128:(n + 1) * 128] = fin[n] * factor
    for n in range(2):
        ok_ref[:, n * 128:(n + 1) * 128] = fin[4 + n] * factor
        ov_ref[:, n * 128:(n + 1) * 128] = fin[6 + n] * factor

    def drain(i):
        p_copy(i // NRC, i % NRC).wait_send()

    loop(4 * NRC, drain)
    loop(2 * NRC, lambda i: a_copy(i // NRC, i % NRC).wait_send())
    loop(NRC, lambda rc: x_copy(rc).wait_send())
    loop(CTX - 1, lambda d: ar_copy(d + 1).wait_send())
    loop(7, lambda d: fin_copy(d + 1).wait_send())
    loop(7, lambda d: sq_copy(d + 1).wait_send())


def per_device(x, nw, doc, q, k, v, w, pg, a):
    any_spec = pl.BlockSpec(memory_space=pl.ANY)
    vmem = pl.BlockSpec(memory_space=pltpu.VMEM)
    dma = pltpu.SemaphoreType.DMA
    return pl.pallas_call(
        kernel,
        out_shape=(
            jax.ShapeDtypeStruct((RANK, QCOLS), F32),
            jax.ShapeDtypeStruct((RANK, KCOLS), F32),
            jax.ShapeDtypeStruct((RANK, KCOLS), F32),
        ),
        in_specs=[any_spec] * 9,
        out_specs=(vmem, vmem, vmem),
        scratch_shapes=[
            pltpu.VMEM((ROWS, WIDTH), BF16),
            pltpu.VMEM((1, WIDTH), BF16),
            pltpu.VMEM((1, WINDOW), jnp.int32),
            pltpu.VMEM((ROWS, QCOLS), BF16),
            pltpu.VMEM((WINDOW, KCOLS), BF16),
            pltpu.VMEM((WINDOW, KCOLS), BF16),
            pltpu.VMEM((8, QCOLS, WIDTH), BF16),
            pltpu.VMEM((ROWS, WIDTH), BF16),
            pltpu.VMEM((WIDTH, 3 * RANK), BF16),
            pltpu.VMEM((4, ROWS, QCOLS), BF16),
            pltpu.VMEM((4, ROWS, QCOLS), F32),
            pltpu.VMEM((4, ROWS, QCOLS), BF16),
            pltpu.VMEM((2, ROWS, QCOLS), BF16),
            pltpu.VMEM((2, ROWS, QCOLS), BF16),
            pltpu.VMEM((ROWS, QCOLS), BF16),
            pltpu.VMEM((ROWS, QCOLS), BF16),
            pltpu.VMEM((4, 32, 128), F32),
            pltpu.VMEM((4, 32, 128), F32),
            pltpu.VMEM((32, 128), F32),
            pltpu.VMEM((32, 128), F32),
            pltpu.VMEM((32, 128), BF16),
            pltpu.VMEM((32, WINDOW), BF16),
            pltpu.VMEM((2, QB, KSPAN), F32),
            pltpu.VMEM((8, QB, KSPAN), F32),
            pltpu.VMEM((8, 16, QB), F32),
            pltpu.VMEM((ROWS, QCOLS), BF16),
            pltpu.VMEM((8, RANK, 128), F32),
            pltpu.VMEM((CTX, RANK, 128), F32),
            pltpu.VMEM((RANK, 128), F32),
            pltpu.VMEM((8, RANK, 128), F32),
            pltpu.VMEM((RANK, 128), F32),
            pltpu.VMEM((8, RANK, 128), F32),
            dma((8,)), dma((8,)), dma((2, 3)), dma((2, 3)),
            dma((4, NRC)), dma((4, NRC)), dma((2, NRC)), dma((2, NRC)), dma((NRC,)), dma((NRC,)),
            dma((4,)), dma((4,)), dma, dma, dma((4,)), dma((4,)), dma((2,)), dma((2,)),
            dma((CTX,)), dma((CTX,)), dma((8,)), dma((8,)), dma((8,)), dma((8,)),
        ],
        compiler_params=pltpu.CompilerParams(
            collective_id=0, has_side_effects=True, vmem_limit_bytes=60 * 1024 * 1024
        ),
        cost_estimate=pl.CostEstimate(
            flops=8_000_000_000, bytes_accessed=10_000_000, transcendentals=3_000_000
        ),
    )(x, nw.reshape(1, WIDTH), doc.reshape(1, ROWS), q, k, v, w, pg, a)


def solution(mesh):
    placed = (
        P("ctx", "tp"),
        P("tp"),
        P("ctx"),
        P("ctx", "tp"),
        P("ctx", "tp"),
        P("ctx", "tp"),
        P(None, "tp"),
        P("ctx", "tp"),
        P("tp", None),
    )
    return jax.shard_map(
        per_device,
        mesh=mesh,
        in_specs=placed,
        out_specs=(P(None, "tp"), P(None, "tp"), P(None, "tp")),
        check_vma=False,
    )
```

```python
import jax
import jax.numpy as jnp
from jax import lax
from jax.experimental import pallas as pl
from jax.experimental.pallas import tpu as pltpu
from jax.sharding import PartitionSpec as P

MODEL_WIDTH = 5376
QUERY_HEADS = 32
KEY_VALUE_HEADS = 16
HEAD_SIZE = 128
LOOKBACK_SPAN = 1024
RANK = 8

CTX = 32
ROWS = 512
WIDTH = 672
QCOLS = 512
KCOLS = 256
WINDOW = 1536
QB = 256
KSPAN = 1280
RC = 128
NRC = ROWS // RC
SCALE = float(MODEL_WIDTH // QUERY_HEADS) ** (-0.5)
LOG2E = 1.4426950408889634

MESH = pl.DeviceIdType.MESH
NT = (((1,), (1,)), ((), ()))
NN = (((1,), (0,)), ((), ()))
F32 = jnp.float32
BF16 = jnp.bfloat16


def dot(a, b, dims=NN):
    return lax.dot_general(a, b, dims, preferred_element_type=F32)


def loop(count, body):
    def step(i, carry):
        body(i)
        return carry

    lax.fori_loop(0, count, step, 0)


def kernel(
    x_ref, nw_ref, doc_ref, q_ref, k_ref, v_ref, w_ref, pg_ref, a_ref,
    out_ref,
    xs, nws, ids, qs, kx, vx, ws, pgt, pgs, am,
    psend, pacc, precv, asend, arecv, xsend, xrecv,
    tmine, trecv, tx_send, tx_recv, lown, lx,
    bias, probs, rv, g, acc, ar, red, fin, sq, sqr,
    load_sem, wload_sem, halo_send, halo_recv,
    p_send, p_recv, a_send, a_recv, x_send, x_recv,
    t1_send, t1_recv, t2_send, t2_recv, t3_send, t3_recv, t4_send, t4_recv,
    ar_send, ar_recv, fin_send, fin_recv, sq_send, sq_recv,
):
    c = lax.axis_index("ctx")
    t = lax.axis_index("tp")
    xh = t // 4
    y = t % 4
    z = c // 4
    low = c % 4
    up = xh * 4 + (y + 1) % 4
    down = xh * 4 + (y + 3) % 4
    across = (t + 4) % 8

    def remote(src, dst, ssem, rsem, cc, tt):
        return pltpu.make_async_remote_copy(
            src_ref=src, dst_ref=dst, send_sem=ssem, recv_sem=rsem,
            device_id=(cc, tt), device_id_type=MESH,
        )

    loads = [
        pltpu.make_async_copy(src, dst, load_sem.at[n])
        for n, (src, dst) in enumerate([
            (x_ref, xs), (nw_ref, nws), (a_ref, am), (pg_ref, pgt), (q_ref, qs),
            (k_ref, kx.at[pl.ds(1024, ROWS), :]), (v_ref, vx.at[pl.ds(1024, ROWS), :]),
            (doc_ref, ids.at[:, pl.ds(1024, ROWS)]),
        ])
    ]
    for copy in loads:
        copy.start()

    def order_of(s):
        first_x = ((s + 1) // 2) % 2
        first_y = 2 + (s // 2) * ((s % 2) * 2 - 1)
        late = s - 4
        late_x = s % 2
        late_y = (1 - late // 2) * (1 + 2 * (s % 2))
        is_late = s // 4
        dx = first_x * (1 - is_late) + late_x * is_late
        dy = first_y * (1 - is_late) + late_y * is_late
        return dx * 4 + (y + dy) % 4

    def wload(s):
        cols = pl.ds(pl.multiple_of(order_of(s) * QCOLS, QCOLS), QCOLS)
        return pltpu.make_async_copy(w_ref.at[:, cols], ws.at[s], wload_sem.at[s])

    loop(8, lambda s: wload(s).start())

    barrier = pltpu.get_barrier_semaphore()

    def greet_ctx(i):
        pl.semaphore_signal(barrier, inc=1, device_id=((c + 1 + i) % CTX, t), device_id_type=MESH)

    def greet_tp(i):
        pl.semaphore_signal(barrier, inc=1, device_id=(c, (t + 1 + i) % 8), device_id_type=MESH)

    loop(CTX - 1, greet_ctx)
    loop(7, greet_tp)

    for copy in loads[:3]:
        copy.wait()
    sel_row = lax.broadcasted_iota(jnp.int32, (32, 3 * RANK), 0)
    sel_col = lax.broadcasted_iota(jnp.int32, (32, 3 * RANK), 1)
    wanted = jnp.where(sel_row < 16, sel_row + 8, jnp.where(sel_row < 24, sel_row - 16, -1))
    select = (wanted == sel_col).astype(BF16)
    maps = dot(select, am[...]) * nws[...].astype(F32).reshape(1, WIDTH)
    maps_hi = maps.astype(BF16)
    maps_lo = (maps - maps_hi.astype(F32)).astype(BF16)
    x_low = xs[...]
    part = dot(maps_hi, x_low) + dot(maps_lo, x_low)
    x_wide = x_low.astype(F32)
    square = x_wide * x_wide
    square_hi = square.astype(BF16)
    square_lo = (square - square_hi.astype(F32)).astype(BF16)
    ones = jnp.ones((RANK, WIDTH), BF16)
    squares = dot(ones, square_hi) + dot(ones, square_lo)
    for n in range(4):
        cols = slice(n * 128, (n + 1) * 128)
        tmine[n, 0:24, :] = part[0:24, cols]
        tmine[n, 24:32, :] = squares[:, cols]

    def rows_of(rc):
        return pl.ds(pl.multiple_of(rc * RC, RC), RC)

    def p_copy(s, rc):
        turn = (y + 1 + 2 * (s % 2)) % 4
        return remote(
            psend.at[s, rows_of(rc), :], precv.at[s, rows_of(rc), :],
            p_send.at[s, rc], p_recv.at[s, rc], c, xh * 4 + turn,
        )

    def early(s):
        wload(s).wait()
        psend[s] = dot(pgs[...], ws[s]).astype(BF16)

    def late(s):
        wload(s + 4).wait()
        pacc[s] = dot(pgs[...], ws[s + 4])

    loads[3].wait()
    pgs[...] = jnp.transpose(pgt[...], (1, 0))
    loop(2, early)

    pl.semaphore_wait(barrier, CTX - 1 + 7)

    def t1_copy(d):
        dest = (y + d) % 4
        return remote(tmine.at[dest], trecv.at[y], t1_send.at[d], t1_recv.at[y], c, xh * 4 + dest)

    def t1_wait(d):
        src = (y + d) % 4
        remote(tmine.at[y], trecv.at[src], t1_send.at[d], t1_recv.at[src], c, t).wait_recv()
        t1_copy(d).wait_send()

    loop(3, lambda d: t1_copy(d + 1).start())

    def halo_copies(n):
        d = n + 1
        dest = (c + d) % CTX
        rows = pl.ds((2 - d) * ROWS, ROWS)
        return [
            remote(k_ref, kx.at[rows, :], halo_send.at[n, 0], halo_recv.at[n, 0], dest, t),
            remote(doc_ref, ids.at[:, rows], halo_send.at[n, 1], halo_recv.at[n, 1], dest, t),
            remote(v_ref, vx.at[rows, :], halo_send.at[n, 2], halo_recv.at[n, 2], dest, t),
        ]

    halos = [halo_copies(0), halo_copies(1)]
    for n in range(2):
        p_copy(n, 0).start()
    for m in range(2):
        for n in range(2):
            halos[n][m].start()
    for n in range(2):
        p_copy(n, 1).start()

    def p_next(s, rc, s_before, rc_before):
        for n in range(2):
            p_copy(s_before + n, rc_before).wait_send()
            p_copy(s + n, rc).start()

    loop(2, lambda s: early(s + 2))
    p_next(0, 2, 0, 0)
    for n in range(2):
        halos[n][2].start()

    loop(3, lambda d: t1_wait(d + 1))
    tsum = tmine[y]
    for d in range(1, 4):
        tsum = tsum + trecv[(y + d) % 4]
    tx_send[...] = tsum
    t2 = remote(tx_send, tx_recv, t2_send, t2_recv, c, across)
    t2.start()

    loop(2, late)
    p_next(0, 3, 0, 1)
    loop(2, lambda s: late(s + 2))
    p_next(2, 0, 0, 2)

    t2.wait()
    tfull = tx_send[...] + tx_recv[...]
    rstd = lax.rsqrt(tfull[24:32, :] * (1.0 / MODEL_WIDTH) + 1e-06)
    lown[...] = (tfull * jnp.concatenate([rstd] * 4, axis=0)).astype(BF16)

    def own_cols(n):
        return pl.ds(pl.multiple_of(1024 + n * 128, 128), 128)

    lx[:, own_cols(y)] = lown[...]

    def t3_copy(d):
        return remote(
            lown, lx.at[:, own_cols(y)], t3_send.at[d], t3_recv.at[y], c, xh * 4 + (y + d) % 4
        )

    def t3_wait(d):
        src = (y + d) % 4
        remote(lown, lx.at[:, own_cols(src)], t3_send.at[d], t3_recv.at[src], c, t).wait_recv()
        t3_copy(d).wait_send()

    loop(3, lambda d: t3_copy(d + 1).start())

    def a_copy(s, rc):
        turn = (y + 1 + 2 * s) % 4
        return remote(
            asend.at[s, rows_of(rc), :], arecv.at[s, rows_of(rc), :],
            a_send.at[s, rc], a_recv.at[s, rc], c, xh * 4 + turn,
        )

    def pass_on(rc):
        for n in range(2):
            p_copy(n, rc).wait_recv()
            asend[n, rows_of(rc), :] = (
                pacc[n, rows_of(rc), :] + precv[n, rows_of(rc), :].astype(F32)
            ).astype(BF16)

    pass_on(0)
    for n in range(2):
        p_copy(n, 3).wait_send()
        a_copy(n, 0).start()

    loop(3, lambda d: t3_wait(d + 1))
    t4s = [
        remote(
            lx.at[pl.ds(0, 16), pl.ds(1024, ROWS)], lx.at[pl.ds(0, 16), pl.ds((1 - n) * ROWS, ROWS)],
            t4_send.at[n], t4_recv.at[n], (c + n + 1) % CTX, t,
        )
        for n in range(2)
    ]
    for copy in t4s:
        copy.start()

    for copy in loads[4:]:
        copy.wait()
    for n in range(2):
        halos[n][0].wait()
        halos[n][1].wait()
    key_at = lax.broadcasted_iota(jnp.int32, (1, WINDOW), 1) + c * ROWS - LOOKBACK_SPAN
    key_ids = jnp.where(key_at < 0, -1, ids[...]).astype(F32)
    own_ids = jnp.broadcast_to(key_ids[:, 1024:1536], (128, ROWS))
    query_ids = jnp.transpose(own_ids, (1, 0))
    row_at = lax.broadcasted_iota(jnp.int32, (QB, 128), 0)
    col_at = lax.broadcasted_iota(jnp.int32, (QB, 128), 1)
    for b in range(2):
        for m in range(KSPAN // 128):
            spacing = 1024 - m * 128 + row_at - col_at
            start = b * QB + m * 128
            allowed = (
                (spacing >= 0)
                & (spacing < LOOKBACK_SPAN)
                & (query_ids[b * QB:(b + 1) * QB, :] == key_ids[:, start:start + 128])
            )
            bias[b, :, m * 128:(m + 1) * 128] = jnp.where(allowed, 0.0, -1e30)

    def parts_of(i):
        h, b = i // 2, i % 2
        q_rows = pl.ds(pl.multiple_of(b * QB, QB), QB)
        k_rows = pl.ds(pl.multiple_of(b * QB, QB), KSPAN)
        h_cols = pl.ds(pl.multiple_of(h * HEAD_SIZE, HEAD_SIZE), HEAD_SIZE)
        g_cols = pl.ds(pl.multiple_of((h // 2) * HEAD_SIZE, HEAD_SIZE), HEAD_SIZE)
        return h, b, q_rows, k_rows, h_cols, g_cols

    def softmax(i):
        h, b, q_rows, k_rows, h_cols, g_cols = parts_of(i)
        scores = dot(qs[q_rows, h_cols], kx[k_rows, g_cols], NT) * (SCALE * LOG2E) + bias[b]
        highest = jnp.max(scores, axis=-1, keepdims=True)
        expons = jnp.exp2(scores - highest)
        total = jnp.sum(expons, axis=-1, keepdims=True)
        probs[i] = expons * (1.0 / total)

    def value_side(i):
        b = i % 2
        lows = lx[0:16, pl.ds(pl.multiple_of(b * QB, QB), KSPAN)]
        rv[i] = dot(lows, probs[i].astype(BF16), NT)

    def x_copy(rc):
        return remote(
            xsend.at[rows_of(rc), :], xrecv.at[rows_of(rc), :],
            x_send.at[rc], x_recv.at[rc], c, across,
        )

    def finish(rc):
        rows = rows_of(rc)
        p_copy(2, rc).wait_recv()
        p_copy(3, rc).wait_recv()
        a_copy(0, rc).wait_recv()
        a_copy(1, rc).wait_recv()
        xsend[rows, :] = (
            pacc[3 - xh, rows, :] + arecv[1 - xh, rows, :].astype(F32)
            + precv[2 + xh, rows, :].astype(F32)
        ).astype(BF16)
        x_copy(rc).start()
        pacc[2 + xh, rows, :] = (
            pacc[2 + xh, rows, :] + arecv[xh, rows, :].astype(F32)
            + precv[3 - xh, rows, :].astype(F32)
        )

    def take(rc):
        rows = rows_of(rc)
        x_copy(rc).wait_recv()
        g[rows, :] = (pacc[2 + xh, rows, :] + xrecv[rows, :].astype(F32)).astype(BF16)

    def backward(b, h):
        i = h * 2 + b
        h, b, q_rows, k_rows, h_cols, g_cols = parts_of(i)
        grad = g[q_rows, h_cols]
        keys = kx[k_rows, g_cols]
        grad_probs = dot(grad, vx[k_rows, g_cols], NT)
        prob = probs[i]
        delta = jnp.sum(prob * grad_probs, axis=-1, keepdims=True)
        grad_scores = (prob * (grad_probs - delta)).astype(BF16)
        lows = lx[0:16, k_rows]
        side_k = (dot(lows, grad_scores, NT) * SCALE).astype(BF16)
        own = lx[16:32, pl.ds(pl.multiple_of(1024 + b * QB, QB), QB)]
        side_q = (dot(own, grad_scores) * SCALE).astype(BF16)
        acc[h] += dot(side_q, keys)[0:8]
        acc[4 + h // 2] += dot(side_k, qs[q_rows, h_cols])[0:8]
        acc[6 + h // 2] += dot(rv[i].astype(BF16), grad)[8:16]

    acc[...] = jnp.zeros_like(acc)
    for n in range(2):
        p_copy(2 + n, 0).wait_send()
        p_copy(2 + n, 1).start()
    loop(3, softmax)
    pass_on(1)
    for n in range(2):
        a_copy(n, 1).start()
    loop(3, lambda i: softmax(i + 3))
    for n in range(2):
        a_copy(n, 0).wait_send()
        p_copy(2 + n, 2).start()
    loop(2, lambda i: softmax(i + 6))
    finish(0)
    pass_on(2)
    for n in range(2):
        p_copy(2 + n, 1).wait_send()
        a_copy(n, 2).start()
    for copy in t4s:
        copy.wait()
    loop(4, value_side)
    finish(1)
    for n in range(2):
        a_copy(n, 1).wait_send()
        p_copy(2 + n, 3).start()
    loop(4, lambda i: value_side(i + 4))
    pass_on(3)
    for n in range(2):
        p_copy(2 + n, 2).wait_send()
        a_copy(n, 3).start()
    for n in range(2):
        halos[n][2].wait()
    loop(2, take)
    loop(4, lambda h: backward(0, h))
    finish(2)
    finish(3)
    loop(2, lambda n: take(n + 2))
    loop(4, lambda h: backward(1, h))

    def ar_copy(d):
        dest = (c + d) % CTX
        return remote(acc.at[dest // 4], ar.at[c], ar_send.at[d], ar_recv.at[c], dest, t)

    def ar_wait(d):
        src = (c + d) % CTX
        remote(acc.at[z], ar.at[src], ar_send.at[d], ar_recv.at[src], c, t).wait_recv()

    loop(CTX - 1, lambda i: ar_copy(16 + (i + 1) // 2 * (2 * (i % 2) - 1)).start())
    ar[c] = acc[z]
    loop(CTX - 1, lambda d: ar_wait(d + 1))
    red[...] = jnp.sum(ar[...], axis=0)

    def fin_copy(d):
        return remote(
            red, fin.at[z], fin_send.at[d], fin_recv.at[z], ((z + d) % 8) * 4 + low, t
        )

    def fin_wait(d):
        src = (z + d) % 8
        remote(red, fin.at[src], fin_send.at[d], fin_recv.at[src], c, t).wait_recv()

    loop(7, lambda i: fin_copy(4 + (i + 1) // 2 * (2 * (i % 2) - 1)).start())
    fin[z] = red[...]
    loop(7, lambda d: fin_wait(d + 1))

    whole = fin[...]
    sq[...] = jnp.sum(whole * whole, axis=0)

    def sq_copy(d):
        return remote(sq, sqr.at[t], sq_send.at[d], sq_recv.at[t], c, (t + d) % 8)

    def sq_wait(d):
        src = (t + d) % 8
        remote(sq, sqr.at[src], sq_send.at[d], sq_recv.at[src], c, t).wait_recv()

    loop(7, lambda d: sq_copy(d + 1).start())
    sqr[t] = sq[...]
    loop(7, lambda d: sq_wait(d + 1))
    squared = jnp.sum(jnp.sum(jnp.sum(sqr[...], axis=0), axis=0, keepdims=True), axis=1, keepdims=True)
    factor = jnp.sqrt(
        float(RANK * (QUERY_HEADS + 2 * KEY_VALUE_HEADS) * HEAD_SIZE) / (squared + 1e-06)
    )
    out_ref[...] = fin[...] * factor

    for n in range(2):
        p_copy(2 + n, 3).wait_send()
        a_copy(n, 2).wait_send()
        a_copy(n, 3).wait_send()
    loop(NRC, lambda rc: x_copy(rc).wait_send())
    loop(CTX - 1, lambda d: ar_copy(d + 1).wait_send())
    loop(7, lambda d: fin_copy(d + 1).wait_send())
    loop(7, lambda d: sq_copy(d + 1).wait_send())


def split(sum_ref, oq_ref, ok_ref, ov_ref):
    for n in range(4):
        oq_ref[:, n * 128:(n + 1) * 128] = sum_ref[n]
    for n in range(2):
        ok_ref[:, n * 128:(n + 1) * 128] = sum_ref[4 + n]
        ov_ref[:, n * 128:(n + 1) * 128] = sum_ref[6 + n]


def per_device(x, nw, doc, q, k, v, w, pg, a):
    any_spec = pl.BlockSpec(memory_space=pl.ANY)
    vmem = pl.BlockSpec(memory_space=pltpu.VMEM)
    dma = pltpu.SemaphoreType.DMA
    summed = pl.pallas_call(
        kernel,
        out_shape=jax.ShapeDtypeStruct((8, RANK, HEAD_SIZE), F32),
        in_specs=[any_spec] * 9,
        out_specs=vmem,
        scratch_shapes=[
            pltpu.VMEM((WIDTH, ROWS), BF16),
            pltpu.VMEM((WIDTH,), BF16),
            pltpu.VMEM((1, WINDOW), jnp.int32),
            pltpu.VMEM((ROWS, QCOLS), BF16),
            pltpu.VMEM((WINDOW, KCOLS), BF16),
            pltpu.VMEM((WINDOW, KCOLS), BF16),
            pltpu.VMEM((8, WIDTH, QCOLS), BF16),
            pltpu.VMEM((WIDTH, ROWS), BF16),
            pltpu.VMEM((ROWS, WIDTH), BF16),
            pltpu.VMEM((3 * RANK, WIDTH), BF16),
            pltpu.VMEM((4, ROWS, QCOLS), BF16),
            pltpu.VMEM((4, ROWS, QCOLS), F32),
            pltpu.VMEM((4, ROWS, QCOLS), BF16),
            pltpu.VMEM((2, ROWS, QCOLS), BF16),
            pltpu.VMEM((2, ROWS, QCOLS), BF16),
            pltpu.VMEM((ROWS, QCOLS), BF16),
            pltpu.VMEM((ROWS, QCOLS), BF16),
            pltpu.VMEM((4, 32, 128), F32),
            pltpu.VMEM((4, 32, 128), F32),
            pltpu.VMEM((32, 128), F32),
            pltpu.VMEM((32, 128), F32),
            pltpu.VMEM((32, 128), BF16),
            pltpu.VMEM((32, WINDOW), BF16),
            pltpu.VMEM((2, QB, KSPAN), F32),
            pltpu.VMEM((8, QB, KSPAN), F32),
            pltpu.VMEM((8, 16, QB), F32),
            pltpu.VMEM((ROWS, QCOLS), BF16),
            pltpu.VMEM((8, RANK, 128), F32),
            pltpu.VMEM((CTX, RANK, 128), F32),
            pltpu.VMEM((RANK, 128), F32),
            pltpu.VMEM((8, RANK, 128), F32),
            pltpu.VMEM((RANK, 128), F32),
            pltpu.VMEM((8, RANK, 128), F32),
            dma((8,)), dma((8,)), dma((2, 3)), dma((2, 3)),
            dma((4, NRC)), dma((4, NRC)), dma((2, NRC)), dma((2, NRC)), dma((NRC,)), dma((NRC,)),
            dma((4,)), dma((4,)), dma, dma, dma((4,)), dma((4,)), dma((2,)), dma((2,)),
            dma((CTX,)), dma((CTX,)), dma((8,)), dma((8,)), dma((8,)), dma((8,)),
        ],
        compiler_params=pltpu.CompilerParams(
            collective_id=0, has_side_effects=True, vmem_limit_bytes=60 * 1024 * 1024
        ),
        cost_estimate=pl.CostEstimate(
            flops=8_000_000_000, bytes_accessed=10_000_000, transcendentals=3_000_000
        ),
    )(x.T, nw, doc.reshape(1, ROWS), q, k, v, w.T, pg.T, a.T)
    return pl.pallas_call(
        split,
        out_shape=(
            jax.ShapeDtypeStruct((RANK, QCOLS), F32),
            jax.ShapeDtypeStruct((RANK, KCOLS), F32),
            jax.ShapeDtypeStruct((RANK, KCOLS), F32),
        ),
        in_specs=[vmem],
        out_specs=(vmem, vmem, vmem),
    )(summed)


def solution(mesh):
    placed = (
        P("ctx", "tp"),
        P("tp"),
        P("ctx"),
        P("ctx", "tp"),
        P("ctx", "tp"),
        P("ctx", "tp"),
        P(None, "tp"),
        P("ctx", "tp"),
        P("tp", None),
    )
    return jax.shard_map(
        per_device,
        mesh=mesh,
        in_specs=placed,
        out_specs=(P(None, "tp"), P(None, "tp"), P(None, "tp")),
        check_vma=False,
    )
```

```python
import jax
import jax.numpy as jnp
from jax import lax
from jax.experimental import pallas as pl
from jax.experimental.pallas import tpu as pltpu
from jax.sharding import PartitionSpec as P

MODEL_WIDTH = 5376
QUERY_HEADS = 32
KEY_VALUE_HEADS = 16
HEAD_SIZE = 128
LOOKBACK_SPAN = 1024
RANK = 8

CTX = 32
ROWS = 512
WIDTH = 672
QCOLS = 512
KCOLS = 256
WINDOW = 1536
KSPAN = 1152
RC = 128
NRC = ROWS // RC
SCALE = float(MODEL_WIDTH // QUERY_HEADS) ** (-0.5)
LOG2E = 1.4426950408889634

MESH = pl.DeviceIdType.MESH
NT = (((1,), (1,)), ((), ()))
NN = (((1,), (0,)), ((), ()))
F32 = jnp.float32
BF16 = jnp.bfloat16


def dot(a, b, dims=NN):
    return lax.dot_general(a, b, dims, preferred_element_type=F32)


def loop(count, body):
    def step(i, carry):
        body(i)
        return carry

    lax.fori_loop(0, count, step, 0)


def kernel(
    x_ref, nw_ref, doc_ref, q_ref, k_ref, v_ref, w_ref, pg_ref, a_ref,
    out_ref,
    xs, nws, ids, qs, kx, vx, ws, pgt, pgs, am,
    psend, pacc, precv, asend, arecv, xsend, xrecv,
    tmine, trecv, tx_send, tx_recv, lown, lx,
    bias, probs, rv, g, acc, ar, red, fin, sq, sqr,
    load_sem, wload_sem, halo_send, halo_recv, id_send, id_recv, known,
    p_send, p_recv, a_send, a_recv, x_send, x_recv,
    t1_send, t1_recv, t2_send, t2_recv, t3_send, t3_recv, t4_send, t4_recv,
    ar_send, ar_recv, fin_send, fin_recv, sq_send, sq_recv,
):
    c = lax.axis_index("ctx")
    t = lax.axis_index("tp")
    xh = t // 4
    y = t % 4
    z = c // 4
    low = c % 4
    up = xh * 4 + (y + 1) % 4
    down = xh * 4 + (y + 3) % 4
    across = (t + 4) % 8

    def remote(src, dst, ssem, rsem, cc, tt):
        return pltpu.make_async_remote_copy(
            src_ref=src, dst_ref=dst, send_sem=ssem, recv_sem=rsem,
            device_id=(cc, tt), device_id_type=MESH,
        )

    loads = [
        pltpu.make_async_copy(src, dst, load_sem.at[n])
        for n, (src, dst) in enumerate([
            (pg_ref, pgt), (x_ref, xs), (nw_ref, nws), (a_ref, am), (q_ref, qs),
            (k_ref, kx.at[pl.ds(1024, ROWS), :]), (v_ref, vx.at[pl.ds(1024, ROWS), :]),
            (doc_ref, ids.at[:, pl.ds(1024, ROWS)]),
        ])
    ]

    def order_of(s):
        first_x = ((s + 1) // 2) % 2
        first_y = 2 + (s // 2) * ((s % 2) * 2 - 1)
        late = s - 4
        late_x = s % 2
        late_y = (1 - late // 2) * (1 + 2 * (s % 2))
        is_late = s // 4
        dx = first_x * (1 - is_late) + late_x * is_late
        dy = first_y * (1 - is_late) + late_y * is_late
        return dx * 4 + (y + dy) % 4

    def wload(s):
        cols = pl.ds(pl.multiple_of(order_of(s) * QCOLS, QCOLS), QCOLS)
        return pltpu.make_async_copy(w_ref.at[:, cols], ws.at[s], wload_sem.at[s])

    loads[0].start()
    loop(2, lambda s: wload(s).start())

    barrier = pltpu.get_barrier_semaphore()

    def greet_tp(i):
        pl.semaphore_signal(barrier, inc=1, device_id=(c, (t + 1 + i) % 8), device_id_type=MESH)

    def meet(sem, d):
        pl.semaphore_signal(sem, inc=1, device_id=((c + d) % CTX, t), device_id_type=MESH)
        pl.semaphore_signal(sem, inc=1, device_id=((c + CTX - d) % CTX, t), device_id_type=MESH)

    loop(7, greet_tp)
    meet(barrier, 1)
    meet(barrier, 2)

    for copy in loads[1:]:
        copy.start()
    loop(6, lambda s: wload(s + 2).start())

    def rows_of(rc):
        return pl.ds(pl.multiple_of(rc * RC, RC), RC)

    def p_copy(s, rc):
        turn = (y + 1 + 2 * (s % 2)) % 4
        return remote(
            psend.at[s, rows_of(rc), :], precv.at[s, rows_of(rc), :],
            p_send.at[s, rc], p_recv.at[s, rc], c, xh * 4 + turn,
        )

    def a_copy(s, rc):
        turn = (y + 1 + 2 * s) % 4
        return remote(
            asend.at[s, rows_of(rc), :], arecv.at[s, rows_of(rc), :],
            a_send.at[s, rc], a_recv.at[s, rc], c, xh * 4 + turn,
        )

    def x_copy(rc):
        return remote(
            xsend.at[rows_of(rc), :], xrecv.at[rows_of(rc), :],
            x_send.at[rc], x_recv.at[rc], c, across,
        )

    def early(s):
        wload(s).wait()
        psend[s] = dot(pgs[...], ws[s]).astype(BF16)

    def late(s):
        wload(s + 4).wait()
        pacc[s] = dot(pgs[...], ws[s + 4])

    def message(k, n):
        if k < 4:
            return p_copy(n, k)
        if k % 2 == 0:
            return p_copy(2 + n, (k - 4) // 2)
        return a_copy(n, (k - 5) // 2)

    def issue(k):
        for n in range(2):
            if k >= 2:
                message(k - 2, n).wait_send()
            message(k, n).start()

    def pass_on(rc):
        for n in range(2):
            p_copy(n, rc).wait_recv()
            asend[n, rows_of(rc), :] = (
                pacc[n, rows_of(rc), :] + precv[n, rows_of(rc), :].astype(F32)
            ).astype(BF16)

    def id_copy(d):
        return remote(
            doc_ref, ids.at[:, pl.ds((2 - d) * ROWS, ROWS)], id_send.at[d - 1], id_recv.at[d - 1],
            (c + d) % CTX, t,
        )

    def kv_copy(m, hop):
        own, window = ((k_ref, kx), (v_ref, vx))[m]
        near = window.at[pl.ds(512, ROWS), :]
        far = window.at[pl.ds(0, ROWS), :]
        return remote(
            near if hop else own, far if hop else near,
            halo_send.at[m, hop], halo_recv.at[m, hop], (c + 1) % CTX, t,
        )

    loads[0].wait()
    pgs[...] = jnp.transpose(pgt[...], (1, 0))
    loop(2, early)
    pl.semaphore_wait(barrier, 7 + 4)

    issue(0)
    kv_copy(0, 0).start()
    issue(1)
    id_copy(1).start()
    id_copy(2).start()
    meet(known.at[0], 2)

    for copy in loads[1:4]:
        copy.wait()
    sel_row = lax.broadcasted_iota(jnp.int32, (32, 3 * RANK), 0)
    sel_col = lax.broadcasted_iota(jnp.int32, (32, 3 * RANK), 1)
    wanted = jnp.where(sel_row < 16, sel_row + 8, jnp.where(sel_row < 24, sel_row - 16, -1))
    select = (wanted == sel_col).astype(BF16)
    maps = dot(select, am[...]) * nws[...].astype(F32).reshape(1, WIDTH)
    maps_hi = maps.astype(BF16)
    maps_lo = (maps - maps_hi.astype(F32)).astype(BF16)
    x_low = xs[...]
    part = dot(maps_hi, x_low) + dot(maps_lo, x_low)
    x_wide = x_low.astype(F32)
    square = x_wide * x_wide
    square_hi = square.astype(BF16)
    square_lo = (square - square_hi.astype(F32)).astype(BF16)
    ones = jnp.ones((RANK, WIDTH), BF16)
    squares = dot(ones, square_hi) + dot(ones, square_lo)
    for n in range(4):
        cols = slice(n * 128, (n + 1) * 128)
        tmine[n, 0:24, :] = part[0:24, cols]
        tmine[n, 24:32, :] = squares[:, cols]

    def t1_copy(d):
        dest = (y + d) % 4
        return remote(tmine.at[dest], trecv.at[y], t1_send.at[d], t1_recv.at[y], c, xh * 4 + dest)

    def t1_wait(d):
        src = (y + d) % 4
        remote(tmine.at[y], trecv.at[src], t1_send.at[d], t1_recv.at[src], c, t).wait_recv()
        t1_copy(d).wait_send()

    loop(3, lambda d: t1_copy(d + 1).start())

    loop(2, lambda s: early(s + 2))
    issue(2)
    loop(2, late)
    kv_copy(0, 0).wait_recv()
    kv_copy(0, 1).start()
    issue(3)
    loop(2, lambda s: late(s + 2))

    loop(3, lambda d: t1_wait(d + 1))
    tsum = tmine[y]
    for d in range(1, 4):
        tsum = tsum + trecv[(y + d) % 4]
    tx_send[...] = tsum
    t2 = remote(tx_send, tx_recv, t2_send, t2_recv, c, across)
    t2.start()
    kv_copy(1, 0).start()
    pl.semaphore_wait(known.at[0], 2)
    meet(known.at[1], 4)

    issue(4)
    pass_on(0)

    for copy in loads[4:]:
        copy.wait()
    id_copy(1).wait()
    id_copy(2).wait()
    key_at = lax.broadcasted_iota(jnp.int32, (1, WINDOW), 1) + c * ROWS - LOOKBACK_SPAN
    key_ids = jnp.where(key_at < 0, -1, ids[...]).astype(F32)
    own_ids = jnp.broadcast_to(key_ids[:, 1024:1536], (128, ROWS))
    query_ids = jnp.transpose(own_ids, (1, 0))
    row_at = lax.broadcasted_iota(jnp.int32, (RC, 128), 0)
    col_at = lax.broadcasted_iota(jnp.int32, (RC, 128), 1)
    for b in range(NRC):
        for m in range(KSPAN // 128):
            start = (b + m) * 128
            spacing = 1024 - m * 128 + row_at - col_at
            allowed = query_ids[b * RC:(b + 1) * RC, :] == key_ids[:, start:start + 128]
            allowed = allowed & (spacing >= 0) & (spacing < LOOKBACK_SPAN)
            bias[b, :, m * 128:(m + 1) * 128] = jnp.where(allowed, 0.0, -1e30)

    def parts_of(i):
        rc, group = i // 2, i % 2
        k_rows = pl.ds(pl.multiple_of(rc * RC, RC), KSPAN)
        g_cols = pl.ds(pl.multiple_of(group * HEAD_SIZE, HEAD_SIZE), HEAD_SIZE)
        return rc, group, k_rows, g_cols

    def both_heads(ref, rc, group):
        return jnp.concatenate([
            ref[rows_of(rc), pl.ds(pl.multiple_of((2 * group + n) * HEAD_SIZE, HEAD_SIZE), HEAD_SIZE)]
            for n in range(2)
        ], axis=0)

    def softmax(i):
        rc, group, k_rows, g_cols = parts_of(i)
        scores = dot(both_heads(qs, rc, group), kx[k_rows, g_cols], NT) * (SCALE * LOG2E)
        scores = (scores.reshape(2, RC, KSPAN) + bias[rc][None]).reshape(2 * RC, KSPAN)
        highest = jnp.max(scores, axis=-1, keepdims=True)
        expons = jnp.exp2(scores - highest)
        total = jnp.sum(expons, axis=-1, keepdims=True)
        probs[i] = expons * (1.0 / total)

    def value_side(i):
        rc, group, k_rows, g_cols = parts_of(i)
        rv[i] = dot(lx[0:16, k_rows], probs[i].astype(BF16), NT)

    def finish(rc):
        rows = rows_of(rc)
        for n in range(2):
            p_copy(2 + n, rc).wait_recv()
            a_copy(n, rc).wait_recv()
        xsend[rows, :] = (
            pacc[3 - xh, rows, :] + arecv[1 - xh, rows, :].astype(F32)
            + precv[2 + xh, rows, :].astype(F32)
        ).astype(BF16)
        x_copy(rc).start()
        pacc[2 + xh, rows, :] = (
            pacc[2 + xh, rows, :] + arecv[xh, rows, :].astype(F32)
            + precv[3 - xh, rows, :].astype(F32)
        )

    def take(rc):
        rows = rows_of(rc)
        x_copy(rc).wait_recv()
        g[rows, :] = (pacc[2 + xh, rows, :] + xrecv[rows, :].astype(F32)).astype(BF16)

    def backward(i):
        rc, group, k_rows, g_cols = parts_of(i)
        grad = both_heads(g, rc, group)
        grad_probs = dot(grad, vx[k_rows, g_cols], NT)
        prob = probs[i]
        delta = jnp.sum(prob * grad_probs, axis=-1, keepdims=True)
        grad_scores = (prob * (grad_probs - delta)).astype(BF16)
        side_k = (dot(lx[0:16, k_rows], grad_scores, NT) * SCALE).astype(BF16)
        own = lx[16:32, pl.ds(pl.multiple_of(1024 + rc * RC, RC), RC)]
        none = jnp.zeros_like(own)
        own_both = jnp.concatenate([
            jnp.concatenate([own, none], axis=1), jnp.concatenate([none, own], axis=1)
        ], axis=0)
        side_q = (dot(own_both, grad_scores) * SCALE).astype(BF16)
        to_q = dot(side_q, kx[k_rows, g_cols])
        acc[2 * group] += to_q[0:8]
        acc[2 * group + 1] += to_q[16:24]
        acc[4 + group] += dot(side_k, both_heads(qs, rc, group))[0:8]
        acc[6 + group] += dot(rv[i].astype(BF16), grad)[8:16]

    acc[...] = jnp.zeros_like(acc)
    issue(5)
    kv_copy(0, 1).wait_recv()
    loop(2, softmax)
    pass_on(1)
    issue(6)

    t2.wait()
    tfull = tx_send[...] + tx_recv[...]
    rstd = lax.rsqrt(tfull[24:32, :] * (1.0 / MODEL_WIDTH) + 1e-06)
    lown[...] = (tfull * jnp.concatenate([rstd] * 4, axis=0)).astype(BF16)

    def own_cols(n):
        return pl.ds(pl.multiple_of(1024 + n * 128, 128), 128)

    lx[:, own_cols(y)] = lown[...]

    def t3_copy(d):
        return remote(
            lown, lx.at[:, own_cols(y)], t3_send.at[d], t3_recv.at[y], c, xh * 4 + (y + d) % 4
        )

    def t3_wait(d):
        src = (y + d) % 4
        remote(lown, lx.at[:, own_cols(src)], t3_send.at[d], t3_recv.at[src], c, t).wait_recv()
        t3_copy(d).wait_send()

    loop(3, lambda d: t3_copy(d + 1).start())
    pl.semaphore_wait(known.at[1], 2)
    meet(known.at[2], 8)

    loop(2, lambda i: softmax(i + 2))
    kv_copy(1, 0).wait_recv()
    kv_copy(1, 1).start()
    issue(7)
    loop(2, lambda i: softmax(i + 4))
    pass_on(2)
    issue(8)

    loop(3, lambda d: t3_wait(d + 1))
    t4s = [
        remote(
            lx.at[pl.ds(0, 16), pl.ds(1024, ROWS)], lx.at[pl.ds(0, 16), pl.ds((1 - n) * ROWS, ROWS)],
            t4_send.at[n], t4_recv.at[n], (c + n + 1) % CTX, t,
        )
        for n in range(2)
    ]
    for copy in t4s:
        copy.start()

    loop(2, lambda i: softmax(i + 6))
    finish(0)
    pass_on(3)
    issue(9)
    issue(10)
    finish(1)
    issue(11)
    for copy in t4s:
        copy.wait()
    kv_copy(1, 1).wait_recv()
    loop(4, value_side)
    take(0)
    loop(2, backward)
    finish(2)
    take(1)
    loop(2, lambda i: backward(i + 2))
    loop(4, lambda i: value_side(i + 4))
    take(2)
    finish(3)
    loop(2, lambda i: backward(i + 4))
    take(3)
    loop(2, lambda i: backward(i + 6))
    pl.semaphore_wait(known.at[2], 2)

    def ar_copy(d):
        dest = (c + d) % CTX
        return remote(acc.at[dest // 4], ar.at[c], ar_send.at[d], ar_recv.at[c], dest, t)

    def ar_wait(d):
        src = (c + d) % CTX
        remote(acc.at[z], ar.at[src], ar_send.at[d], ar_recv.at[src], c, t).wait_recv()

    loop(CTX - 1, lambda i: ar_copy(16 + (i + 1) // 2 * (2 * (i % 2) - 1)).start())
    ar[c] = acc[z]
    loop(CTX - 1, lambda d: ar_wait(d + 1))
    red[...] = jnp.sum(ar[...], axis=0)

    def fin_copy(d):
        return remote(
            red, fin.at[z], fin_send.at[d], fin_recv.at[z], ((z + d) % 8) * 4 + low, t
        )

    def fin_wait(d):
        src = (z + d) % 8
        remote(red, fin.at[src], fin_send.at[d], fin_recv.at[src], c, t).wait_recv()

    loop(7, lambda i: fin_copy(4 + (i + 1) // 2 * (2 * (i % 2) - 1)).start())
    fin[z] = red[...]
    loop(7, lambda d: fin_wait(d + 1))

    whole = fin[...]
    sq[...] = jnp.sum(whole * whole, axis=0)

    def sq_copy(d):
        return remote(sq, sqr.at[t], sq_send.at[d], sq_recv.at[t], c, (t + d) % 8)

    def sq_wait(d):
        src = (t + d) % 8
        remote(sq, sqr.at[src], sq_send.at[d], sq_recv.at[src], c, t).wait_recv()

    loop(7, lambda d: sq_copy(d + 1).start())
    sqr[t] = sq[...]
    loop(7, lambda d: sq_wait(d + 1))
    squared = jnp.sum(jnp.sum(jnp.sum(sqr[...], axis=0), axis=0, keepdims=True), axis=1, keepdims=True)
    factor = jnp.sqrt(
        float(RANK * (QUERY_HEADS + 2 * KEY_VALUE_HEADS) * HEAD_SIZE) / (squared + 1e-06)
    )
    out_ref[...] = fin[...] * factor

    for k in range(10, 12):
        for n in range(2):
            message(k, n).wait_send()
    for n in range(4):
        kv_copy(n // 2, n % 2).wait_send()
    loop(NRC, lambda rc: x_copy(rc).wait_send())
    loop(CTX - 1, lambda d: ar_copy(d + 1).wait_send())
    loop(7, lambda d: fin_copy(d + 1).wait_send())
    loop(7, lambda d: sq_copy(d + 1).wait_send())


def split(sum_ref, oq_ref, ok_ref, ov_ref):
    for n in range(4):
        oq_ref[:, n * 128:(n + 1) * 128] = sum_ref[n]
    for n in range(2):
        ok_ref[:, n * 128:(n + 1) * 128] = sum_ref[4 + n]
        ov_ref[:, n * 128:(n + 1) * 128] = sum_ref[6 + n]


def per_device(x, nw, doc, q, k, v, w, pg, a):
    any_spec = pl.BlockSpec(memory_space=pl.ANY)
    vmem = pl.BlockSpec(memory_space=pltpu.VMEM)
    dma = pltpu.SemaphoreType.DMA
    summed = pl.pallas_call(
        kernel,
        out_shape=jax.ShapeDtypeStruct((8, RANK, HEAD_SIZE), F32),
        in_specs=[any_spec] * 9,
        out_specs=vmem,
        scratch_shapes=[
            pltpu.VMEM((WIDTH, ROWS), BF16),
            pltpu.VMEM((WIDTH,), BF16),
            pltpu.VMEM((1, WINDOW), jnp.int32),
            pltpu.VMEM((ROWS, QCOLS), BF16),
            pltpu.VMEM((WINDOW, KCOLS), BF16),
            pltpu.VMEM((WINDOW, KCOLS), BF16),
            pltpu.VMEM((8, WIDTH, QCOLS), BF16),
            pltpu.VMEM((WIDTH, ROWS), BF16),
            pltpu.VMEM((ROWS, WIDTH), BF16),
            pltpu.VMEM((3 * RANK, WIDTH), BF16),
            pltpu.VMEM((4, ROWS, QCOLS), BF16),
            pltpu.VMEM((4, ROWS, QCOLS), F32),
            pltpu.VMEM((4, ROWS, QCOLS), BF16),
            pltpu.VMEM((2, ROWS, QCOLS), BF16),
            pltpu.VMEM((2, ROWS, QCOLS), BF16),
            pltpu.VMEM((ROWS, QCOLS), BF16),
            pltpu.VMEM((ROWS, QCOLS), BF16),
            pltpu.VMEM((4, 32, 128), F32),
            pltpu.VMEM((4, 32, 128), F32),
            pltpu.VMEM((32, 128), F32),
            pltpu.VMEM((32, 128), F32),
            pltpu.VMEM((32, 128), BF16),
            pltpu.VMEM((32, WINDOW), BF16),
            pltpu.VMEM((NRC, RC, KSPAN), F32),
            pltpu.VMEM((8, 2 * RC, KSPAN), F32),
            pltpu.VMEM((8, 16, 2 * RC), F32),
            pltpu.VMEM((ROWS, QCOLS), BF16),
            pltpu.VMEM((8, RANK, 128), F32),
            pltpu.VMEM((CTX, RANK, 128), F32),
            pltpu.VMEM((RANK, 128), F32),
            pltpu.VMEM((8, RANK, 128), F32),
            pltpu.VMEM((RANK, 128), F32),
            pltpu.VMEM((8, RANK, 128), F32),
            dma((8,)), dma((8,)), dma((2, 2)), dma((2, 2)), dma((2,)), dma((2,)),
            pltpu.SemaphoreType.REGULAR((3,)),
            dma((4, NRC)), dma((4, NRC)), dma((2, NRC)), dma((2, NRC)), dma((NRC,)), dma((NRC,)),
            dma((4,)), dma((4,)), dma, dma, dma((4,)), dma((4,)), dma((2,)), dma((2,)),
            dma((CTX,)), dma((CTX,)), dma((8,)), dma((8,)), dma((8,)), dma((8,)),
        ],
        compiler_params=pltpu.CompilerParams(
            collective_id=0, has_side_effects=True, vmem_limit_bytes=60 * 1024 * 1024
        ),
        cost_estimate=pl.CostEstimate(
            flops=8_000_000_000, bytes_accessed=10_000_000, transcendentals=3_000_000
        ),
    )(x.T, nw, doc.reshape(1, ROWS), q, k, v, w.T, pg.T, a.T)
    return pl.pallas_call(
        split,
        out_shape=(
            jax.ShapeDtypeStruct((RANK, QCOLS), F32),
            jax.ShapeDtypeStruct((RANK, KCOLS), F32),
            jax.ShapeDtypeStruct((RANK, KCOLS), F32),
        ),
        in_specs=[vmem],
        out_specs=(vmem, vmem, vmem),
    )(summed)


def solution(mesh):
    placed = (
        P("ctx", "tp"),
        P("tp"),
        P("ctx"),
        P("ctx", "tp"),
        P("ctx", "tp"),
        P("ctx", "tp"),
        P(None, "tp"),
        P("ctx", "tp"),
        P("tp", None),
    )
    return jax.shard_map(
        per_device,
        mesh=mesh,
        in_specs=placed,
        out_specs=(P(None, "tp"), P(None, "tp"), P(None, "tp")),
        check_vma=False,
    )
```

```python
import jax
import jax.numpy as jnp
from jax import lax
from jax.experimental import pallas as pl
from jax.experimental.pallas import tpu as pltpu
from jax.sharding import PartitionSpec as P

MODEL_WIDTH = 5376
QUERY_HEADS = 32
KEY_VALUE_HEADS = 16
HEAD_SIZE = 128
LOOKBACK_SPAN = 1024
RANK = 8

CTX = 32
ROWS = 512
WIDTH = 672
QCOLS = 512
KCOLS = 256
WINDOW = 1536
KSPAN = 1152
RC = 128
NRC = ROWS // RC
SCALE = float(MODEL_WIDTH // QUERY_HEADS) ** (-0.5)
LOG2E = 1.4426950408889634

MESH = pl.DeviceIdType.MESH
NT = (((1,), (1,)), ((), ()))
NN = (((1,), (0,)), ((), ()))
F32 = jnp.float32
BF16 = jnp.bfloat16


def dot(a, b, dims=NN):
    return lax.dot_general(a, b, dims, preferred_element_type=F32)


def loop(count, body):
    def step(i, carry):
        body(i)
        return carry

    lax.fori_loop(0, count, step, 0)


def kernel(
    x_ref, nw_ref, doc_ref, q_ref, k_ref, v_ref, w_ref, pg_ref, a_ref,
    out_ref,
    xs, nws, ids, qs, kx, vx, ws, pgt, pgs, am,
    psend, pacc, precv, asend, arecv, xsend, xrecv,
    bsend, zrecv, zbuf, ssend, srecv, fsend, frecv,
    tmine, trecv, tx_send, tx_recv, lown, lx,
    bias, probs, rv, g, acc, ar, red, fin, sq, sqr,
    load_sem, wload_sem, halo_send, halo_recv, id_send, id_recv, known,
    z_send, z_recv, s_send, s_recv, f_send, f_recv,
    p_send, p_recv, a_send, a_recv, x_send, x_recv,
    t1_send, t1_recv, t2_send, t2_recv, t3_send, t3_recv, t4_send, t4_recv,
    ar_send, ar_recv, fin_send, fin_recv, sq_send, sq_recv,
):
    c = lax.axis_index("ctx")
    t = lax.axis_index("tp")
    xh = t // 4
    y = t % 4
    z = c // 4
    low = c % 4
    up = xh * 4 + (y + 1) % 4
    down = xh * 4 + (y + 3) % 4
    across = (t + 4) % 8

    def remote(src, dst, ssem, rsem, cc, tt):
        return pltpu.make_async_remote_copy(
            src_ref=src, dst_ref=dst, send_sem=ssem, recv_sem=rsem,
            device_id=(cc, tt), device_id_type=MESH,
        )

    barrier = pltpu.get_barrier_semaphore()

    def greet_y(d):
        pl.semaphore_signal(
            barrier, inc=1, device_id=(c, xh * 4 + (y + d) % 4), device_id_type=MESH
        )

    def meet(sem, d):
        pl.semaphore_signal(sem, inc=1, device_id=((c + d) % CTX, t), device_id_type=MESH)
        pl.semaphore_signal(sem, inc=1, device_id=((c + CTX - d) % CTX, t), device_id_type=MESH)

    for d in (2, 1, 3):
        greet_y(d)
    pl.semaphore_signal(barrier, inc=1, device_id=(c, across), device_id_type=MESH)
    meet(barrier, 1)
    meet(barrier, 2)

    loads = [
        pltpu.make_async_copy(src, dst, load_sem.at[n])
        for n, (src, dst) in enumerate([
            (pg_ref, pgt), (x_ref, xs), (nw_ref, nws), (a_ref, am), (q_ref, qs),
            (k_ref, kx.at[pl.ds(1024, ROWS), :]), (v_ref, vx.at[pl.ds(1024, ROWS), :]),
            (doc_ref, ids.at[:, pl.ds(1024, ROWS)]),
        ])
    ]

    def order_of(s):
        first_x = ((s + 1) // 2) % 2
        first_y = 2 + (s // 2) * ((s % 2) * 2 - 1)
        late = s - 4
        late_x = s % 2
        late_y = (1 - late // 2) * (1 + 2 * (s % 2))
        is_late = s // 4
        dx = first_x * (1 - is_late) + late_x * is_late
        dy = first_y * (1 - is_late) + late_y * is_late
        return dx * 4 + (y + dy) % 4

    def wload(s):
        cols = pl.ds(pl.multiple_of(order_of(s) * QCOLS, QCOLS), QCOLS)
        return pltpu.make_async_copy(w_ref.at[:, cols], ws.at[s], wload_sem.at[s])

    loads[0].start()
    loop(2, lambda s: wload(s).start())

    for copy in loads[1:]:
        copy.start()
    loop(6, lambda s: wload(s + 2).start())

    def rows_of(rc):
        return pl.ds(pl.multiple_of(rc * RC, RC), RC)

    def p_copy(s, rc):
        turn = (y + 1 + 2 * (s % 2)) % 4
        return remote(
            psend.at[s, rows_of(rc), :], precv.at[s, rows_of(rc), :],
            p_send.at[s, rc], p_recv.at[s, rc], c, xh * 4 + turn,
        )

    def a_copy(s, rc):
        turn = (y + 1 + 2 * s) % 4
        return remote(
            asend.at[s, rows_of(rc), :], arecv.at[s, rows_of(rc), :],
            a_send.at[s, rc], a_recv.at[s, rc], c, xh * 4 + turn,
        )

    def x_copy(rc):
        return remote(
            xsend.at[rows_of(rc), :], xrecv.at[rows_of(rc), :],
            x_send.at[rc], x_recv.at[rc], c, across,
        )

    def early(s):
        wload(s).wait()
        psend[s] = dot(pgs[...], ws[s]).astype(BF16)

    def late(s):
        wload(s + 4).wait()
        pacc[s] = dot(pgs[...], ws[s + 4])

    last = pl.ds((NRC - 1) * RC, RC)

    def x_part(m):
        src = (
            psend.at[1 - xh, last, :], psend.at[2 + xh, last, :], bsend.at[0], bsend.at[1]
        )[m]
        slot = (0, 1 + xh, 2 - xh, 3)[m]
        return remote(src, zrecv.at[slot], z_send.at[m], z_recv.at[slot], c, across)

    def x_part_wait(slot):
        remote(bsend.at[0], zrecv.at[slot], z_send.at[0], z_recv.at[slot], c, t).wait_recv()

    def s_copy(n):
        return remote(
            ssend.at[n], srecv.at[n], s_send.at[n], s_recv.at[n], c, xh * 4 + (y + 1 + 2 * n) % 4
        )

    def f_copy(n):
        return remote(
            fsend.at[n], frecv.at[n], f_send.at[n], f_recv.at[n], c, xh * 4 + (y + 1 + 2 * n) % 4
        )

    def message(k, n):
        return (
            lambda: p_copy(n, 0), lambda: p_copy(n, 1), lambda: p_copy(n, 2),
            lambda: p_copy(2 + n, 0), lambda: a_copy(n, 0), lambda: s_copy(n),
            lambda: p_copy(2 + n, 1), lambda: a_copy(n, 1),
            lambda: p_copy(2 + n, 2), lambda: a_copy(n, 2), lambda: f_copy(n),
        )[k]()

    def issue(k):
        for n in range(2):
            if k >= 2:
                message(k - 2, n).wait_send()
            message(k, n).start()

    def pass_on(rc):
        for n in range(2):
            p_copy(n, rc).wait_recv()
            asend[n, rows_of(rc), :] = (
                pacc[n, rows_of(rc), :] + precv[n, rows_of(rc), :].astype(F32)
            ).astype(BF16)

    def id_copy(d):
        return remote(
            doc_ref, ids.at[:, pl.ds((2 - d) * ROWS, ROWS)], id_send.at[d - 1], id_recv.at[d - 1],
            (c + d) % CTX, t,
        )

    def kv_copy(m, hop):
        own, window = ((k_ref, kx), (v_ref, vx))[m]
        near = window.at[pl.ds(512, ROWS), :]
        far = window.at[pl.ds(0, ROWS), :]
        return remote(
            near if hop else own, far if hop else near,
            halo_send.at[m, hop], halo_recv.at[m, hop], (c + 1) % CTX, t,
        )

    loads[0].wait()
    pgs[...] = jnp.transpose(pgt[...], (1, 0))
    loop(2, early)
    pl.semaphore_wait(barrier, 4 + 4)

    issue(0)
    x_part(0).start()
    kv_copy(0, 0).start()
    issue(1)
    id_copy(1).start()
    id_copy(2).start()
    meet(known.at[0], 2)
    pl.semaphore_signal(known.at[3], inc=1, device_id=(c, across), device_id_type=MESH)

    for copy in loads[1:4]:
        copy.wait()
    sel_row = lax.broadcasted_iota(jnp.int32, (32, 3 * RANK), 0)
    sel_col = lax.broadcasted_iota(jnp.int32, (32, 3 * RANK), 1)
    wanted = jnp.where(sel_row < 16, sel_row + 8, jnp.where(sel_row < 24, sel_row - 16, -1))
    select = (wanted == sel_col).astype(BF16)
    maps = dot(select, am[...]) * nws[...].astype(F32).reshape(1, WIDTH)
    maps_hi = maps.astype(BF16)
    maps_lo = (maps - maps_hi.astype(F32)).astype(BF16)
    x_low = xs[...]
    part = dot(maps_hi, x_low) + dot(maps_lo, x_low)
    x_wide = x_low.astype(F32)
    square = x_wide * x_wide
    square_hi = square.astype(BF16)
    square_lo = (square - square_hi.astype(F32)).astype(BF16)
    ones = jnp.ones((RANK, WIDTH), BF16)
    squares = dot(ones, square_hi) + dot(ones, square_lo)
    for n in range(4):
        cols = slice(n * 128, (n + 1) * 128)
        tmine[n, 0:24, :] = part[0:24, cols]
        tmine[n, 24:32, :] = squares[:, cols]

    def t1_copy(d):
        dest = (y + d) % 4
        return remote(tmine.at[dest], trecv.at[y], t1_send.at[d], t1_recv.at[y], c, xh * 4 + dest)

    def t1_wait(d):
        src = (y + d) % 4
        remote(tmine.at[y], trecv.at[src], t1_send.at[d], t1_recv.at[src], c, t).wait_recv()
        t1_copy(d).wait_send()

    loop(3, lambda d: t1_copy(d + 1).start())

    loop(2, lambda s: early(s + 2))
    issue(2)
    loop(2, late)
    bsend[0] = pacc[1 - xh, last, :].astype(BF16)

    loop(3, lambda d: t1_wait(d + 1))
    tsum = tmine[y]
    for d in range(1, 4):
        tsum = tsum + trecv[(y + d) % 4]
    tx_send[...] = tsum
    t2 = remote(tx_send, tx_recv, t2_send, t2_recv, c, across)
    t2.start()
    loop(2, lambda s: late(s + 2))
    bsend[1] = pacc[3 - xh, last, :].astype(BF16)
    kv_copy(0, 0).wait_recv()
    kv_copy(0, 1).start()
    issue(3)
    x_part(1).start()
    x_part(2).start()
    pl.semaphore_wait(known.at[0], 2)
    meet(known.at[1], 4)
    pass_on(0)
    issue(4)
    x_part(3).start()
    kv_copy(1, 0).start()

    t2.wait()
    tfull = tx_send[...] + tx_recv[...]
    rstd = lax.rsqrt(tfull[24:32, :] * (1.0 / MODEL_WIDTH) + 1e-06)
    lown[...] = (tfull * jnp.concatenate([rstd] * 4, axis=0)).astype(BF16)

    def own_cols(n):
        return pl.ds(pl.multiple_of(1024 + n * 128, 128), 128)

    lx[:, own_cols(y)] = lown[...]

    def t3_copy(d):
        return remote(
            lown, lx.at[:, own_cols(y)], t3_send.at[d], t3_recv.at[y], c, xh * 4 + (y + d) % 4
        )

    def t3_wait(d):
        src = (y + d) % 4
        remote(lown, lx.at[:, own_cols(src)], t3_send.at[d], t3_recv.at[src], c, t).wait_recv()
        t3_copy(d).wait_send()

    loop(3, lambda d: t3_copy(d + 1).start())
    for copy in loads[4:]:
        copy.wait()
    id_copy(1).wait()
    id_copy(2).wait()
    key_at = lax.broadcasted_iota(jnp.int32, (1, WINDOW), 1) + c * ROWS - LOOKBACK_SPAN
    key_ids = jnp.where(key_at < 0, -1, ids[...]).astype(F32)
    own_ids = jnp.broadcast_to(key_ids[:, 1024:1536], (128, ROWS))
    query_ids = jnp.transpose(own_ids, (1, 0))
    row_at = lax.broadcasted_iota(jnp.int32, (RC, 128), 0)
    col_at = lax.broadcasted_iota(jnp.int32, (RC, 128), 1)
    for b in range(NRC):
        for m in range(KSPAN // 128):
            start = (b + m) * 128
            spacing = 1024 - m * 128 + row_at - col_at
            allowed = query_ids[b * RC:(b + 1) * RC, :] == key_ids[:, start:start + 128]
            allowed = allowed & (spacing >= 0) & (spacing < LOOKBACK_SPAN)
            bias[b, :, m * 128:(m + 1) * 128] = jnp.where(allowed, 0.0, -1e30)

    def parts_of(i):
        rc, group = i // 2, i % 2
        k_rows = pl.ds(pl.multiple_of(rc * RC, RC), KSPAN)
        g_cols = pl.ds(pl.multiple_of(group * HEAD_SIZE, HEAD_SIZE), HEAD_SIZE)
        return rc, group, k_rows, g_cols

    def both_heads(ref, rc, group):
        return jnp.concatenate([
            ref[rows_of(rc), pl.ds(pl.multiple_of((2 * group + n) * HEAD_SIZE, HEAD_SIZE), HEAD_SIZE)]
            for n in range(2)
        ], axis=0)

    def softmax(i):
        rc, group, k_rows, g_cols = parts_of(i)
        scores = dot(both_heads(qs, rc, group), kx[k_rows, g_cols], NT) * (SCALE * LOG2E)
        scores = (scores.reshape(2, RC, KSPAN) + bias[rc][None]).reshape(2 * RC, KSPAN)
        highest = jnp.max(scores, axis=-1, keepdims=True)
        expons = jnp.exp2(scores - highest)
        total = jnp.sum(expons, axis=-1, keepdims=True)
        probs[i] = expons * (1.0 / total)

    def value_side(i):
        rc, group, k_rows, g_cols = parts_of(i)
        rv[i] = dot(lx[0:16, k_rows], probs[i].astype(BF16), NT)

    def finish(rc):
        rows = rows_of(rc)
        for n in range(2):
            p_copy(2 + n, rc).wait_recv()
            a_copy(n, rc).wait_recv()
        xsend[rows, :] = (
            pacc[3 - xh, rows, :] + arecv[1 - xh, rows, :].astype(F32)
            + precv[2 + xh, rows, :].astype(F32)
        ).astype(BF16)
        x_copy(rc).start()
        pacc[2 + xh, rows, :] = (
            pacc[2 + xh, rows, :] + arecv[xh, rows, :].astype(F32)
            + precv[3 - xh, rows, :].astype(F32)
        )

    def take(rc):
        rows = rows_of(rc)
        x_copy(rc).wait_recv()
        g[rows, :] = (pacc[2 + xh, rows, :] + xrecv[rows, :].astype(F32)).astype(BF16)

    def backward(i):
        rc, group, k_rows, g_cols = parts_of(i)
        grad = both_heads(g, rc, group)
        grad_probs = dot(grad, vx[k_rows, g_cols], NT)
        prob = probs[i]
        delta = jnp.sum(prob * grad_probs, axis=-1, keepdims=True)
        grad_scores = (prob * (grad_probs - delta)).astype(BF16)
        side_k = (dot(lx[0:16, k_rows], grad_scores, NT) * SCALE).astype(BF16)
        own = lx[16:32, pl.ds(pl.multiple_of(1024 + rc * RC, RC), RC)]
        none = jnp.zeros_like(own)
        own_both = jnp.concatenate([
            jnp.concatenate([own, none], axis=1), jnp.concatenate([none, own], axis=1)
        ], axis=0)
        side_q = (dot(own_both, grad_scores) * SCALE).astype(BF16)
        to_q = dot(side_q, kx[k_rows, g_cols])
        acc[2 * group] += to_q[0:8]
        acc[2 * group + 1] += to_q[16:24]
        acc[4 + group] += dot(side_k, both_heads(qs, rc, group))[0:8]
        acc[6 + group] += dot(rv[i].astype(BF16), grad)[8:16]

    acc[...] = jnp.zeros_like(acc)
    x_part_wait(0)
    far = psend[xh, last, :].astype(F32) + zrecv[0].astype(F32)
    ssend[0] = far[:, 0:256].astype(BF16)
    ssend[1] = far[:, 256:512].astype(BF16)
    issue(5)
    kv_copy(0, 1).wait_recv()
    loop(2, softmax)
    pass_on(1)
    issue(6)

    loop(3, lambda d: t3_wait(d + 1))
    t4s = [
        remote(
            lx.at[pl.ds(0, 16), pl.ds(1024, ROWS)], lx.at[pl.ds(0, 16), pl.ds((1 - n) * ROWS, ROWS)],
            t4_send.at[n], t4_recv.at[n], (c + n + 1) % CTX, t,
        )
        for n in range(2)
    ]
    for copy in t4s:
        copy.start()

    pl.semaphore_wait(known.at[1], 2)
    meet(known.at[2], 8)
    loop(2, lambda i: softmax(i + 2))
    kv_copy(1, 0).wait_recv()
    kv_copy(1, 1).start()
    issue(7)
    loop(2, lambda i: softmax(i + 4))
    pass_on(2)
    issue(8)
    finish(0)
    loop(2, lambda i: softmax(i + 6))

    for slot in range(1, 4):
        x_part_wait(slot)
    zbuf[2 - xh] = psend[3 - xh, last, :].astype(F32) + zrecv[2 - xh].astype(F32)
    zbuf[1 + xh] = pacc[xh, last, :] + zrecv[1 + xh].astype(F32)
    zbuf[3] = pacc[2 + xh, last, :] + zrecv[3].astype(F32)
    for n in range(2):
        s_copy(n).wait_recv()
        passed = slice(n * 256, (n + 1) * 256)
        direct = slice((1 - n) * 256, (2 - n) * 256)
        fsend[n, :, passed] = (zbuf[1 + n, :, passed] + srecv[n].astype(F32)).astype(BF16)
        fsend[n, :, direct] = zbuf[1 + n, :, direct].astype(BF16)

    issue(9)
    for copy in t4s:
        copy.wait()
    loop(4, value_side)
    kv_copy(1, 1).wait_recv()
    issue(10)
    take(0)
    finish(1)
    loop(2, backward)
    loop(4, lambda i: value_side(i + 4))
    finish(2)
    take(1)
    loop(2, lambda i: backward(i + 2))
    for n in range(2):
        f_copy(n).wait_recv()
    g[last, :] = (zbuf[3] + frecv[0].astype(F32) + frecv[1].astype(F32)).astype(BF16)
    loop(2, lambda i: backward(i + 6))
    take(2)
    loop(2, lambda i: backward(i + 4))
    pl.semaphore_wait(known.at[2], 2)
    pl.semaphore_wait(known.at[3], 1)

    def ar_copy(d):
        dest = (c + d) % CTX
        return remote(acc.at[dest // 4], ar.at[c], ar_send.at[d], ar_recv.at[c], dest, t)

    def ar_wait(d):
        src = (c + d) % CTX
        remote(acc.at[z], ar.at[src], ar_send.at[d], ar_recv.at[src], c, t).wait_recv()

    loop(CTX - 1, lambda i: ar_copy(16 + (i + 1) // 2 * (2 * (i % 2) - 1)).start())
    ar[c] = acc[z]
    loop(CTX - 1, lambda d: ar_wait(d + 1))
    red[...] = jnp.sum(ar[...], axis=0)

    def spread(i):
        return 4 + (i + 1) // 2 * (2 * (i % 2) - 1)

    def fin_copy(d):
        return remote(
            red, fin.at[z], fin_send.at[d], fin_recv.at[z], ((z + d) % 8) * 4 + low, t
        )

    def fin_wait(d):
        src = (z + d) % 8
        remote(red, fin.at[src], fin_send.at[d], fin_recv.at[src], c, t).wait_recv()

    loop(7, lambda i: fin_copy(spread(i)).start())
    fin[z] = red[...]
    loop(7, lambda d: fin_wait(d + 1))

    whole = fin[...]
    sq[...] = jnp.sum(whole * whole, axis=0)

    def sq_copy(d):
        return remote(sq, sqr.at[t], sq_send.at[d], sq_recv.at[t], c, (t + d) % 8)

    def sq_wait(d):
        src = (t + d) % 8
        remote(sq, sqr.at[src], sq_send.at[d], sq_recv.at[src], c, t).wait_recv()

    loop(7, lambda d: sq_copy(d + 1).start())
    sqr[t] = sq[...]
    loop(7, lambda d: sq_wait(d + 1))
    squared = jnp.sum(jnp.sum(jnp.sum(sqr[...], axis=0), axis=0, keepdims=True), axis=1, keepdims=True)
    factor = jnp.sqrt(
        float(RANK * (QUERY_HEADS + 2 * KEY_VALUE_HEADS) * HEAD_SIZE) / (squared + 1e-06)
    )
    out_ref[...] = fin[...] * factor

    for k in range(9, 11):
        for n in range(2):
            message(k, n).wait_send()
    for n in range(4):
        kv_copy(n // 2, n % 2).wait_send()
    for m in range(4):
        x_part(m).wait_send()
    loop(NRC - 1, lambda rc: x_copy(rc).wait_send())
    loop(CTX - 1, lambda d: ar_copy(d + 1).wait_send())
    loop(7, lambda d: fin_copy(d + 1).wait_send())
    loop(7, lambda d: sq_copy(d + 1).wait_send())


def split(sum_ref, oq_ref, ok_ref, ov_ref):
    for n in range(4):
        oq_ref[:, n * 128:(n + 1) * 128] = sum_ref[n]
    for n in range(2):
        ok_ref[:, n * 128:(n + 1) * 128] = sum_ref[4 + n]
        ov_ref[:, n * 128:(n + 1) * 128] = sum_ref[6 + n]


def per_device(x, nw, doc, q, k, v, w, pg, a):
    any_spec = pl.BlockSpec(memory_space=pl.ANY)
    vmem = pl.BlockSpec(memory_space=pltpu.VMEM)
    dma = pltpu.SemaphoreType.DMA
    summed = pl.pallas_call(
        kernel,
        out_shape=jax.ShapeDtypeStruct((8, RANK, HEAD_SIZE), F32),
        in_specs=[any_spec] * 9,
        out_specs=vmem,
        scratch_shapes=[
            pltpu.VMEM((WIDTH, ROWS), BF16),
            pltpu.VMEM((WIDTH,), BF16),
            pltpu.VMEM((1, WINDOW), jnp.int32),
            pltpu.VMEM((ROWS, QCOLS), BF16),
            pltpu.VMEM((WINDOW, KCOLS), BF16),
            pltpu.VMEM((WINDOW, KCOLS), BF16),
            pltpu.VMEM((8, WIDTH, QCOLS), BF16),
            pltpu.VMEM((WIDTH, ROWS), BF16),
            pltpu.VMEM((ROWS, WIDTH), BF16),
            pltpu.VMEM((3 * RANK, WIDTH), BF16),
            pltpu.VMEM((4, ROWS, QCOLS), BF16),
            pltpu.VMEM((4, ROWS, QCOLS), F32),
            pltpu.VMEM((4, ROWS, QCOLS), BF16),
            pltpu.VMEM((2, ROWS, QCOLS), BF16),
            pltpu.VMEM((2, ROWS, QCOLS), BF16),
            pltpu.VMEM((ROWS, QCOLS), BF16),
            pltpu.VMEM((ROWS, QCOLS), BF16),
            pltpu.VMEM((2, RC, QCOLS), BF16),
            pltpu.VMEM((4, RC, QCOLS), BF16),
            pltpu.VMEM((4, RC, QCOLS), F32),
            pltpu.VMEM((2, RC, QCOLS // 2), BF16),
            pltpu.VMEM((2, RC, QCOLS // 2), BF16),
            pltpu.VMEM((2, RC, QCOLS), BF16),
            pltpu.VMEM((2, RC, QCOLS), BF16),
            pltpu.VMEM((4, 32, 128), F32),
            pltpu.VMEM((4, 32, 128), F32),
            pltpu.VMEM((32, 128), F32),
            pltpu.VMEM((32, 128), F32),
            pltpu.VMEM((32, 128), BF16),
            pltpu.VMEM((32, WINDOW), BF16),
            pltpu.VMEM((NRC, RC, KSPAN), F32),
            pltpu.VMEM((8, 2 * RC, KSPAN), F32),
            pltpu.VMEM((8, 16, 2 * RC), F32),
            pltpu.VMEM((ROWS, QCOLS), BF16),
            pltpu.VMEM((8, RANK, 128), F32),
            pltpu.VMEM((CTX, RANK, 128), F32),
            pltpu.VMEM((RANK, 128), F32),
            pltpu.VMEM((8, RANK, 128), F32),
            pltpu.VMEM((RANK, 128), F32),
            pltpu.VMEM((8, RANK, 128), F32),
            dma((8,)), dma((8,)), dma((2, 2)), dma((2, 2)), dma((2,)), dma((2,)),
            pltpu.SemaphoreType.REGULAR((4,)),
            dma((4,)), dma((4,)), dma((2,)), dma((2,)), dma((2,)), dma((2,)),
            dma((4, NRC)), dma((4, NRC)), dma((2, NRC)), dma((2, NRC)), dma((NRC,)), dma((NRC,)),
            dma((4,)), dma((4,)), dma, dma, dma((4,)), dma((4,)), dma((2,)), dma((2,)),
            dma((CTX,)), dma((CTX,)), dma((8,)), dma((8,)), dma((8,)), dma((8,)),
        ],
        compiler_params=pltpu.CompilerParams(
            collective_id=0, has_side_effects=True, vmem_limit_bytes=60 * 1024 * 1024
        ),
        cost_estimate=pl.CostEstimate(
            flops=8_000_000_000, bytes_accessed=10_000_000, transcendentals=3_000_000
        ),
    )(x.T, nw, doc.reshape(1, ROWS), q, k, v, w.T, pg.T, a.T)
    return pl.pallas_call(
        split,
        out_shape=(
            jax.ShapeDtypeStruct((RANK, QCOLS), F32),
            jax.ShapeDtypeStruct((RANK, KCOLS), F32),
            jax.ShapeDtypeStruct((RANK, KCOLS), F32),
        ),
        in_specs=[vmem],
        out_specs=(vmem, vmem, vmem),
    )(summed)


def solution(mesh):
    placed = (
        P("ctx", "tp"),
        P("tp"),
        P("ctx"),
        P("ctx", "tp"),
        P("ctx", "tp"),
        P("ctx", "tp"),
        P(None, "tp"),
        P("ctx", "tp"),
        P("tp", None),
    )
    return jax.shard_map(
        per_device,
        mesh=mesh,
        in_specs=placed,
        out_specs=(P(None, "tp"), P(None, "tp"), P(None, "tp")),
        check_vma=False,
    )
```

```python
import jax
import jax.numpy as jnp
from jax import lax
from jax.experimental import pallas as pl
from jax.experimental.pallas import tpu as pltpu
from jax.sharding import PartitionSpec as P

MODEL_WIDTH = 5376
QUERY_HEADS = 32
KEY_VALUE_HEADS = 16
HEAD_SIZE = 128
LOOKBACK_SPAN = 1024
RANK = 8

CTX = 32
ROWS = 512
WIDTH = 672
QCOLS = 512
KCOLS = 256
WINDOW = 1536
KSPAN = 1152
RC = 128
NRC = ROWS // RC
SCALE = float(MODEL_WIDTH // QUERY_HEADS) ** (-0.5)
LOG2E = 1.4426950408889634

MESH = pl.DeviceIdType.MESH
NT = (((1,), (1,)), ((), ()))
NN = (((1,), (0,)), ((), ()))
F32 = jnp.float32
BF16 = jnp.bfloat16


def dot(a, b, dims=NN):
    return lax.dot_general(a, b, dims, preferred_element_type=F32)


def loop(count, body):
    def step(i, carry):
        body(i)
        return carry

    lax.fori_loop(0, count, step, 0)


def kernel(
    x_ref, nw_ref, doc_ref, q_ref, k_ref, v_ref, w_ref, pg_ref, a_ref,
    out_ref,
    xs, nws, ids, qs, kx, vx, ws, pgt, pgs, am,
    psend, pacc, precv, asend, arecv, xsend, xrecv,
    bsend, zrecv, zbuf, ssend, srecv, fsend, frecv,
    tmine, trecv, tx_send, tx_recv, lown, lx,
    bias, probs, rv, g, acc, ar, red, fin, sq, sqr,
    load_sem, wload_sem, halo_send, halo_recv, id_send, id_recv, known,
    z_send, z_recv, s_send, s_recv, f_send, f_recv,
    p_send, p_recv, a_send, a_recv, x_send, x_recv,
    t1_send, t1_recv, t2_send, t2_recv, t3_send, t3_recv, t4_send, t4_recv,
    ar_send, ar_recv, fin_send, fin_recv, sq_send, sq_recv,
):
    c = lax.axis_index("ctx")
    t = lax.axis_index("tp")
    xh = t // 4
    y = t % 4
    z = c // 4
    low = c % 4
    up = xh * 4 + (y + 1) % 4
    down = xh * 4 + (y + 3) % 4
    across = (t + 4) % 8

    def remote(src, dst, ssem, rsem, cc, tt):
        return pltpu.make_async_remote_copy(
            src_ref=src, dst_ref=dst, send_sem=ssem, recv_sem=rsem,
            device_id=(cc, tt), device_id_type=MESH,
        )

    loads = [
        pltpu.make_async_copy(src, dst, load_sem.at[n])
        for n, (src, dst) in enumerate([
            (pg_ref, pgt), (x_ref, xs), (nw_ref, nws), (a_ref, am), (q_ref, qs),
            (k_ref, kx.at[pl.ds(1024, ROWS), :]), (v_ref, vx.at[pl.ds(1024, ROWS), :]),
            (doc_ref, ids.at[:, pl.ds(1024, ROWS)]),
        ])
    ]

    def order_of(s):
        first_x = ((s + 1) // 2) % 2
        first_y = 2 + (s // 2) * ((s % 2) * 2 - 1)
        late = s - 4
        late_x = s % 2
        late_y = (1 - late // 2) * (1 + 2 * (s % 2))
        is_late = s // 4
        dx = first_x * (1 - is_late) + late_x * is_late
        dy = first_y * (1 - is_late) + late_y * is_late
        return dx * 4 + (y + dy) % 4

    def wload(s):
        cols = pl.ds(pl.multiple_of(order_of(s) * QCOLS, QCOLS), QCOLS)
        return pltpu.make_async_copy(w_ref.at[:, cols], ws.at[s], wload_sem.at[s])

    loads[0].start()
    loop(2, lambda s: wload(s).start())

    barrier = pltpu.get_barrier_semaphore()

    def greet_y(d):
        pl.semaphore_signal(
            barrier, inc=1, device_id=(c, xh * 4 + (y + d) % 4), device_id_type=MESH
        )

    def meet(sem, d):
        pl.semaphore_signal(sem, inc=1, device_id=((c + d) % CTX, t), device_id_type=MESH)
        pl.semaphore_signal(sem, inc=1, device_id=((c + CTX - d) % CTX, t), device_id_type=MESH)

    for d in (2, 1, 3):
        greet_y(d)
    pl.semaphore_signal(barrier, inc=1, device_id=(c, across), device_id_type=MESH)
    meet(barrier, 1)
    meet(barrier, 2)


    def rows_of(rc):
        return pl.ds(pl.multiple_of(rc * RC, RC), RC)

    def p_copy(s, rc):
        turn = (y + 1 + 2 * (s % 2)) % 4
        return remote(
            psend.at[s, rows_of(rc), :], precv.at[s, rows_of(rc), :],
            p_send.at[s, rc], p_recv.at[s, rc], c, xh * 4 + turn,
        )

    def a_copy(s, rc):
        turn = (y + 1 + 2 * s) % 4
        return remote(
            asend.at[s, rows_of(rc), :], arecv.at[s, rows_of(rc), :],
            a_send.at[s, rc], a_recv.at[s, rc], c, xh * 4 + turn,
        )

    def x_copy(rc):
        return remote(
            xsend.at[rows_of(rc), :], xrecv.at[rows_of(rc), :],
            x_send.at[rc], x_recv.at[rc], c, across,
        )

    def early(s):
        wload(s).wait()
        psend[s] = dot(pgs[...], ws[s]).astype(BF16)

    def late(s):
        wload(s + 4).wait()
        pacc[s] = dot(pgs[...], ws[s + 4])

    last = pl.ds((NRC - 1) * RC, RC)

    def x_part(m):
        src = (
            psend.at[1 - xh, last, :], psend.at[2 + xh, last, :], bsend.at[0], bsend.at[1]
        )[m]
        slot = (0, 1 + xh, 2 - xh, 3)[m]
        return remote(src, zrecv.at[slot], z_send.at[m], z_recv.at[slot], c, across)

    def x_part_wait(slot):
        remote(bsend.at[0], zrecv.at[slot], z_send.at[0], z_recv.at[slot], c, t).wait_recv()

    def s_copy(n):
        return remote(
            ssend.at[n], srecv.at[n], s_send.at[n], s_recv.at[n], c, xh * 4 + (y + 1 + 2 * n) % 4
        )

    def f_copy(n):
        return remote(
            fsend.at[n], frecv.at[n], f_send.at[n], f_recv.at[n], c, xh * 4 + (y + 1 + 2 * n) % 4
        )

    def message(k, n):
        return (
            lambda: p_copy(n, 0), lambda: p_copy(n, 1), lambda: p_copy(n, 2),
            lambda: p_copy(2 + n, 0), lambda: a_copy(n, 0), lambda: s_copy(n),
            lambda: p_copy(2 + n, 1), lambda: a_copy(n, 1),
            lambda: p_copy(2 + n, 2), lambda: a_copy(n, 2), lambda: f_copy(n),
        )[k]()

    def issue(k):
        for n in range(2):
            if k >= 4:
                message(k - 4, n).wait_send()
            message(k, n).start()

    def pass_on(rc):
        for n in range(2):
            p_copy(n, rc).wait_recv()
            asend[n, rows_of(rc), :] = (
                pacc[n, rows_of(rc), :] + precv[n, rows_of(rc), :].astype(F32)
            ).astype(BF16)

    def id_copy(d):
        return remote(
            doc_ref, ids.at[:, pl.ds((2 - d) * ROWS, ROWS)], id_send.at[d - 1], id_recv.at[d - 1],
            (c + d) % CTX, t,
        )

    def kv_copy(m, hop):
        own, window = ((k_ref, kx), (v_ref, vx))[m]
        near = window.at[pl.ds(512, ROWS), :]
        far = window.at[pl.ds(0, ROWS), :]
        return remote(
            near if hop else own, far if hop else near,
            halo_send.at[m, hop], halo_recv.at[m, hop], (c + 1) % CTX, t,
        )

    loads[0].wait()
    pgs[0:RC, :] = jnp.transpose(pgt[:, 0:RC], (1, 0))

    def first(s):
        wload(s).wait()
        psend[s, 0:RC, :] = dot(pgs[0:RC, :], ws[s]).astype(BF16)

    loop(2, first)
    pl.semaphore_wait(barrier, 4 + 4)

    issue(0)
    for copy in loads[1:]:
        copy.start()
    loop(6, lambda s: wload(s + 2).start())
    pgs[RC:ROWS, :] = jnp.transpose(pgt[:, RC:ROWS], (1, 0))

    def second(s):
        psend[s, RC:ROWS, :] = dot(pgs[RC:ROWS, :], ws[s]).astype(BF16)

    loop(2, second)
    x_part(0).start()
    kv_copy(0, 0).start()
    issue(1)
    id_copy(1).start()
    id_copy(2).start()
    kv_copy(1, 0).start()
    meet(known.at[0], 2)
    pl.semaphore_signal(known.at[3], inc=1, device_id=(c, across), device_id_type=MESH)

    for copy in loads[1:4]:
        copy.wait()
    sel_row = lax.broadcasted_iota(jnp.int32, (32, 3 * RANK), 0)
    sel_col = lax.broadcasted_iota(jnp.int32, (32, 3 * RANK), 1)
    wanted = jnp.where(sel_row < 16, sel_row + 8, jnp.where(sel_row < 24, sel_row - 16, -1))
    select = (wanted == sel_col).astype(BF16)
    maps = dot(select, am[...]) * nws[...].astype(F32).reshape(1, WIDTH)
    maps_hi = maps.astype(BF16)
    maps_lo = (maps - maps_hi.astype(F32)).astype(BF16)
    x_low = xs[...]
    part = dot(maps_hi, x_low) + dot(maps_lo, x_low)
    x_wide = x_low.astype(F32)
    square = x_wide * x_wide
    square_hi = square.astype(BF16)
    square_lo = (square - square_hi.astype(F32)).astype(BF16)
    ones = jnp.ones((RANK, WIDTH), BF16)
    squares = dot(ones, square_hi) + dot(ones, square_lo)
    for n in range(4):
        cols = slice(n * 128, (n + 1) * 128)
        tmine[n, 0:24, :] = part[0:24, cols]
        tmine[n, 24:32, :] = squares[:, cols]

    def t1_copy(d):
        dest = (y + d) % 4
        return remote(tmine.at[dest], trecv.at[y], t1_send.at[d], t1_recv.at[y], c, xh * 4 + dest)

    def t1_wait(d):
        src = (y + d) % 4
        remote(tmine.at[y], trecv.at[src], t1_send.at[d], t1_recv.at[src], c, t).wait_recv()
        t1_copy(d).wait_send()

    loop(3, lambda d: t1_copy(d + 1).start())

    loop(2, lambda s: early(s + 2))
    issue(2)
    loop(2, late)
    bsend[0] = pacc[1 - xh, last, :].astype(BF16)

    loop(3, lambda d: t1_wait(d + 1))
    tsum = tmine[y]
    for d in range(1, 4):
        tsum = tsum + trecv[(y + d) % 4]
    tx_send[...] = tsum
    t2 = remote(tx_send, tx_recv, t2_send, t2_recv, c, across)
    t2.start()
    loop(2, lambda s: late(s + 2))
    bsend[1] = pacc[3 - xh, last, :].astype(BF16)
    issue(3)
    kv_copy(0, 0).wait_recv()
    kv_copy(0, 1).start()
    x_part(1).start()
    x_part(2).start()
    pl.semaphore_wait(known.at[0], 2)
    meet(known.at[1], 4)
    pass_on(0)
    issue(4)
    x_part(3).start()

    t2.wait()
    tfull = tx_send[...] + tx_recv[...]
    rstd = lax.rsqrt(tfull[24:32, :] * (1.0 / MODEL_WIDTH) + 1e-06)
    lown[...] = (tfull * jnp.concatenate([rstd] * 4, axis=0)).astype(BF16)

    def own_cols(n):
        return pl.ds(pl.multiple_of(1024 + n * 128, 128), 128)

    lx[:, own_cols(y)] = lown[...]

    def t3_copy(d):
        return remote(
            lown, lx.at[:, own_cols(y)], t3_send.at[d], t3_recv.at[y], c, xh * 4 + (y + d) % 4
        )

    def t3_wait(d):
        src = (y + d) % 4
        remote(lown, lx.at[:, own_cols(src)], t3_send.at[d], t3_recv.at[src], c, t).wait_recv()
        t3_copy(d).wait_send()

    loop(3, lambda d: t3_copy(d + 1).start())
    for copy in loads[4:]:
        copy.wait()
    id_copy(1).wait()
    id_copy(2).wait()
    key_at = lax.broadcasted_iota(jnp.int32, (1, WINDOW), 1) + c * ROWS - LOOKBACK_SPAN
    key_ids = jnp.where(key_at < 0, -1, ids[...]).astype(F32)
    own_ids = jnp.broadcast_to(key_ids[:, 1024:1536], (128, ROWS))
    query_ids = jnp.transpose(own_ids, (1, 0))
    row_at = lax.broadcasted_iota(jnp.int32, (RC, 128), 0)
    col_at = lax.broadcasted_iota(jnp.int32, (RC, 128), 1)
    for b in range(NRC):
        for m in range(KSPAN // 128):
            start = (b + m) * 128
            spacing = 1024 - m * 128 + row_at - col_at
            allowed = query_ids[b * RC:(b + 1) * RC, :] == key_ids[:, start:start + 128]
            allowed = allowed & (spacing >= 0) & (spacing < LOOKBACK_SPAN)
            bias[b, :, m * 128:(m + 1) * 128] = jnp.where(allowed, 0.0, -1e30)

    def parts_of(i):
        rc, group = i // 2, i % 2
        k_rows = pl.ds(pl.multiple_of(rc * RC, RC), KSPAN)
        g_cols = pl.ds(pl.multiple_of(group * HEAD_SIZE, HEAD_SIZE), HEAD_SIZE)
        return rc, group, k_rows, g_cols

    def both_heads(ref, rc, group):
        return jnp.concatenate([
            ref[rows_of(rc), pl.ds(pl.multiple_of((2 * group + n) * HEAD_SIZE, HEAD_SIZE), HEAD_SIZE)]
            for n in range(2)
        ], axis=0)

    def softmax(i):
        rc, group, k_rows, g_cols = parts_of(i)
        scores = dot(both_heads(qs, rc, group), kx[k_rows, g_cols], NT) * (SCALE * LOG2E)
        scores = (scores.reshape(2, RC, KSPAN) + bias[rc][None]).reshape(2 * RC, KSPAN)
        highest = jnp.max(scores, axis=-1, keepdims=True)
        expons = jnp.exp2(scores - highest)
        total = jnp.sum(expons, axis=-1, keepdims=True)
        probs[i] = expons * (1.0 / total)

    def value_side(i):
        rc, group, k_rows, g_cols = parts_of(i)
        rv[i] = dot(lx[0:16, k_rows], probs[i].astype(BF16), NT)

    def finish(rc):
        rows = rows_of(rc)
        for n in range(2):
            p_copy(2 + n, rc).wait_recv()
            a_copy(n, rc).wait_recv()
        xsend[rows, :] = (
            pacc[3 - xh, rows, :] + arecv[1 - xh, rows, :].astype(F32)
            + precv[2 + xh, rows, :].astype(F32)
        ).astype(BF16)
        x_copy(rc).start()
        pacc[2 + xh, rows, :] = (
            pacc[2 + xh, rows, :] + arecv[xh, rows, :].astype(F32)
            + precv[3 - xh, rows, :].astype(F32)
        )

    def take(rc):
        rows = rows_of(rc)
        x_copy(rc).wait_recv()
        g[rows, :] = (pacc[2 + xh, rows, :] + xrecv[rows, :].astype(F32)).astype(BF16)

    def backward(i):
        rc, group, k_rows, g_cols = parts_of(i)
        grad = both_heads(g, rc, group)
        grad_probs = dot(grad, vx[k_rows, g_cols], NT)
        prob = probs[i]
        delta = jnp.sum(prob * grad_probs, axis=-1, keepdims=True)
        grad_scores = (prob * (grad_probs - delta)).astype(BF16)
        side_k = (dot(lx[0:16, k_rows], grad_scores, NT) * SCALE).astype(BF16)
        own = lx[16:32, pl.ds(pl.multiple_of(1024 + rc * RC, RC), RC)]
        none = jnp.zeros_like(own)
        own_both = jnp.concatenate([
            jnp.concatenate([own, none], axis=1), jnp.concatenate([none, own], axis=1)
        ], axis=0)
        side_q = (dot(own_both, grad_scores) * SCALE).astype(BF16)
        to_q = dot(side_q, kx[k_rows, g_cols])
        acc[2 * group] += to_q[0:8]
        acc[2 * group + 1] += to_q[16:24]
        acc[4 + group] += dot(side_k, both_heads(qs, rc, group))[0:8]
        acc[6 + group] += dot(rv[i].astype(BF16), grad)[8:16]

    acc[...] = jnp.zeros_like(acc)
    x_part_wait(0)
    far = psend[xh, last, :].astype(F32) + zrecv[0].astype(F32)
    ssend[0] = far[:, 0:256].astype(BF16)
    ssend[1] = far[:, 256:512].astype(BF16)
    issue(5)
    kv_copy(1, 0).wait_recv()
    kv_copy(1, 1).start()
    kv_copy(0, 1).wait_recv()
    loop(2, softmax)
    pass_on(1)
    issue(6)

    loop(3, lambda d: t3_wait(d + 1))
    t4s = [
        remote(
            lx.at[pl.ds(0, 16), pl.ds(1024, ROWS)], lx.at[pl.ds(0, 16), pl.ds((1 - n) * ROWS, ROWS)],
            t4_send.at[n], t4_recv.at[n], (c + n + 1) % CTX, t,
        )
        for n in range(2)
    ]
    for copy in t4s:
        copy.start()

    pl.semaphore_wait(known.at[1], 2)
    meet(known.at[2], 8)
    loop(2, lambda i: softmax(i + 2))
    issue(7)
    loop(2, lambda i: softmax(i + 4))
    pass_on(2)
    issue(8)
    finish(0)
    loop(2, lambda i: softmax(i + 6))

    for slot in range(1, 4):
        x_part_wait(slot)
    zbuf[2 - xh] = psend[3 - xh, last, :].astype(F32) + zrecv[2 - xh].astype(F32)
    zbuf[1 + xh] = pacc[xh, last, :] + zrecv[1 + xh].astype(F32)
    zbuf[3] = pacc[2 + xh, last, :] + zrecv[3].astype(F32)
    for n in range(2):
        s_copy(n).wait_recv()
        passed = slice(n * 256, (n + 1) * 256)
        direct = slice((1 - n) * 256, (2 - n) * 256)
        fsend[n, :, passed] = (zbuf[1 + n, :, passed] + srecv[n].astype(F32)).astype(BF16)
        fsend[n, :, direct] = zbuf[1 + n, :, direct].astype(BF16)

    issue(9)
    issue(10)
    for copy in t4s:
        copy.wait()
    loop(4, value_side)
    kv_copy(1, 1).wait_recv()
    take(0)
    finish(1)
    loop(2, backward)
    loop(4, lambda i: value_side(i + 4))
    finish(2)
    take(1)
    loop(2, lambda i: backward(i + 2))
    for n in range(2):
        f_copy(n).wait_recv()
    g[last, :] = (zbuf[3] + frecv[0].astype(F32) + frecv[1].astype(F32)).astype(BF16)
    loop(2, lambda i: backward(i + 6))
    take(2)
    loop(2, lambda i: backward(i + 4))
    pl.semaphore_wait(known.at[2], 2)
    pl.semaphore_wait(known.at[3], 1)

    def ar_copy(d):
        dest = (c + d) % CTX
        return remote(acc.at[dest // 4], ar.at[c], ar_send.at[d], ar_recv.at[c], dest, t)

    def ar_wait(d):
        src = (c + d) % CTX
        remote(acc.at[z], ar.at[src], ar_send.at[d], ar_recv.at[src], c, t).wait_recv()

    loop(CTX - 1, lambda i: ar_copy(16 + (i + 1) // 2 * (2 * (i % 2) - 1)).start())
    ar[c] = acc[z]
    for k in range(7, 11):
        for n in range(2):
            message(k, n).wait_send()
    for n in range(4):
        kv_copy(n // 2, n % 2).wait_send()
    for m in range(4):
        x_part(m).wait_send()
    loop(NRC - 1, lambda rc: x_copy(rc).wait_send())
    loop(CTX - 1, lambda d: ar_wait(d + 1))
    red[...] = jnp.sum(ar[...], axis=0)

    def spread(i):
        return 4 + (i + 1) // 2 * (2 * (i % 2) - 1)

    def fin_copy(d):
        return remote(
            red, fin.at[z], fin_send.at[d], fin_recv.at[z], ((z + d) % 8) * 4 + low, t
        )

    def fin_wait(d):
        src = (z + d) % 8
        remote(red, fin.at[src], fin_send.at[d], fin_recv.at[src], c, t).wait_recv()

    loop(7, lambda i: fin_copy(spread(i)).start())
    fin[z] = red[...]
    loop(CTX - 1, lambda d: ar_copy(d + 1).wait_send())
    loop(7, lambda d: fin_wait(d + 1))

    whole = fin[...]
    sq[...] = jnp.sum(whole * whole, axis=0)

    def sq_copy(d):
        return remote(sq, sqr.at[t], sq_send.at[d], sq_recv.at[t], c, (t + d) % 8)

    def sq_wait(d):
        src = (t + d) % 8
        remote(sq, sqr.at[src], sq_send.at[d], sq_recv.at[src], c, t).wait_recv()

    loop(7, lambda d: sq_copy(d + 1).start())
    sqr[t] = sq[...]
    loop(7, lambda d: fin_copy(d + 1).wait_send())
    loop(7, lambda d: sq_wait(d + 1))
    squared = jnp.sum(jnp.sum(jnp.sum(sqr[...], axis=0), axis=0, keepdims=True), axis=1, keepdims=True)
    factor = jnp.sqrt(
        float(RANK * (QUERY_HEADS + 2 * KEY_VALUE_HEADS) * HEAD_SIZE) / (squared + 1e-06)
    )
    out_ref[...] = fin[...] * factor
    loop(7, lambda d: sq_copy(d + 1).wait_send())


def split(sum_ref, oq_ref, ok_ref, ov_ref):
    for n in range(4):
        oq_ref[:, n * 128:(n + 1) * 128] = sum_ref[n]
    for n in range(2):
        ok_ref[:, n * 128:(n + 1) * 128] = sum_ref[4 + n]
        ov_ref[:, n * 128:(n + 1) * 128] = sum_ref[6 + n]


def per_device(x, nw, doc, q, k, v, w, pg, a):
    any_spec = pl.BlockSpec(memory_space=pl.ANY)
    vmem = pl.BlockSpec(memory_space=pltpu.VMEM)
    dma = pltpu.SemaphoreType.DMA
    summed = pl.pallas_call(
        kernel,
        out_shape=jax.ShapeDtypeStruct((8, RANK, HEAD_SIZE), F32),
        in_specs=[any_spec] * 9,
        out_specs=vmem,
        scratch_shapes=[
            pltpu.VMEM((WIDTH, ROWS), BF16),
            pltpu.VMEM((WIDTH,), BF16),
            pltpu.VMEM((1, WINDOW), jnp.int32),
            pltpu.VMEM((ROWS, QCOLS), BF16),
            pltpu.VMEM((WINDOW, KCOLS), BF16),
            pltpu.VMEM((WINDOW, KCOLS), BF16),
            pltpu.VMEM((8, WIDTH, QCOLS), BF16),
            pltpu.VMEM((WIDTH, ROWS), BF16),
            pltpu.VMEM((ROWS, WIDTH), BF16),
            pltpu.VMEM((3 * RANK, WIDTH), BF16),
            pltpu.VMEM((4, ROWS, QCOLS), BF16),
            pltpu.VMEM((4, ROWS, QCOLS), F32),
            pltpu.VMEM((4, ROWS, QCOLS), BF16),
            pltpu.VMEM((2, ROWS, QCOLS), BF16),
            pltpu.VMEM((2, ROWS, QCOLS), BF16),
            pltpu.VMEM((ROWS, QCOLS), BF16),
            pltpu.VMEM((ROWS, QCOLS), BF16),
            pltpu.VMEM((2, RC, QCOLS), BF16),
            pltpu.VMEM((4, RC, QCOLS), BF16),
            pltpu.VMEM((4, RC, QCOLS), F32),
            pltpu.VMEM((2, RC, QCOLS // 2), BF16),
            pltpu.VMEM((2, RC, QCOLS // 2), BF16),
            pltpu.VMEM((2, RC, QCOLS), BF16),
            pltpu.VMEM((2, RC, QCOLS), BF16),
            pltpu.VMEM((4, 32, 128), F32),
            pltpu.VMEM((4, 32, 128), F32),
            pltpu.VMEM((32, 128), F32),
            pltpu.VMEM((32, 128), F32),
            pltpu.VMEM((32, 128), BF16),
            pltpu.VMEM((32, WINDOW), BF16),
            pltpu.VMEM((NRC, RC, KSPAN), F32),
            pltpu.VMEM((8, 2 * RC, KSPAN), F32),
            pltpu.VMEM((8, 16, 2 * RC), F32),
            pltpu.VMEM((ROWS, QCOLS), BF16),
            pltpu.VMEM((8, RANK, 128), F32),
            pltpu.VMEM((CTX, RANK, 128), F32),
            pltpu.VMEM((RANK, 128), F32),
            pltpu.VMEM((8, RANK, 128), F32),
            pltpu.VMEM((RANK, 128), F32),
            pltpu.VMEM((8, RANK, 128), F32),
            dma((8,)), dma((8,)), dma((2, 2)), dma((2, 2)), dma((2,)), dma((2,)),
            pltpu.SemaphoreType.REGULAR((4,)),
            dma((4,)), dma((4,)), dma((2,)), dma((2,)), dma((2,)), dma((2,)),
            dma((4, NRC)), dma((4, NRC)), dma((2, NRC)), dma((2, NRC)), dma((NRC,)), dma((NRC,)),
            dma((4,)), dma((4,)), dma, dma, dma((4,)), dma((4,)), dma((2,)), dma((2,)),
            dma((CTX,)), dma((CTX,)), dma((8,)), dma((8,)), dma((8,)), dma((8,)),
        ],
        compiler_params=pltpu.CompilerParams(
            collective_id=0, has_side_effects=True, vmem_limit_bytes=60 * 1024 * 1024
        ),
        cost_estimate=pl.CostEstimate(
            flops=8_000_000_000, bytes_accessed=10_000_000, transcendentals=3_000_000
        ),
    )(x.T, nw, doc.reshape(1, ROWS), q, k, v, w.T, pg.T, a.T)
    return pl.pallas_call(
        split,
        out_shape=(
            jax.ShapeDtypeStruct((RANK, QCOLS), F32),
            jax.ShapeDtypeStruct((RANK, KCOLS), F32),
            jax.ShapeDtypeStruct((RANK, KCOLS), F32),
        ),
        in_specs=[vmem],
        out_specs=(vmem, vmem, vmem),
    )(summed)


def solution(mesh):
    placed = (
        P("ctx", "tp"),
        P("tp"),
        P("ctx"),
        P("ctx", "tp"),
        P("ctx", "tp"),
        P("ctx", "tp"),
        P(None, "tp"),
        P("ctx", "tp"),
        P("tp", None),
    )
    return jax.shard_map(
        per_device,
        mesh=mesh,
        in_specs=placed,
        out_specs=(P(None, "tp"), P(None, "tp"), P(None, "tp")),
        check_vma=False,
    )
```

```python
import jax
import jax.numpy as jnp
from jax import lax
from jax.experimental import pallas as pl
from jax.experimental.pallas import tpu as pltpu
from jax.sharding import PartitionSpec as P

MODEL_WIDTH = 5376
QUERY_HEADS = 32
KEY_VALUE_HEADS = 16
HEAD_SIZE = 128
LOOKBACK_SPAN = 1024
RANK = 8

CTX = 32
ROWS = 512
WIDTH = 672
QCOLS = 512
KCOLS = 256
WINDOW = 1536
KSPAN = 1152
RC = 128
NRC = ROWS // RC
SCALE = float(MODEL_WIDTH // QUERY_HEADS) ** (-0.5)
LOG2E = 1.4426950408889634

MESH = pl.DeviceIdType.MESH
NT = (((1,), (1,)), ((), ()))
NN = (((1,), (0,)), ((), ()))
F32 = jnp.float32
BF16 = jnp.bfloat16


def dot(a, b, dims=NN):
    return lax.dot_general(a, b, dims, preferred_element_type=F32)


def loop(count, body):
    def step(i, carry):
        body(i)
        return carry

    lax.fori_loop(0, count, step, 0)


def kernel(
    x_ref, nw_ref, doc_ref, q_ref, k_ref, v_ref, w_ref, pg_ref, a_ref,
    out_ref,
    xs, nws, ids, qs, kx, vx, ws, pgt, pgs, am,
    psend, pacc, precv, asend, arecv, xsend, xrecv,
    bsend, zrecv, zbuf, ssend, srecv, fsend, frecv,
    tmine, trecv, tx_send, tx_recv, lown, lx,
    bias, probs, rv, g, acc, ar, red, fin, sq, sqr,
    load_sem, wload_sem, halo_send, halo_recv, id_send, id_recv, known,
    z_send, z_recv, s_send, s_recv, f_send, f_recv,
    p_send, p_recv, a_send, a_recv, x_send, x_recv,
    t1_send, t1_recv, t2_send, t2_recv, t3_send, t3_recv, t4_send, t4_recv,
    ar_send, ar_recv, fin_send, fin_recv, sq_send, sq_recv,
):
    c = lax.axis_index("ctx")
    t = lax.axis_index("tp")
    xh = t // 4
    y = t % 4
    z = c // 4
    low = c % 4
    up = xh * 4 + (y + 1) % 4
    down = xh * 4 + (y + 3) % 4
    across = (t + 4) % 8

    def remote(src, dst, ssem, rsem, cc, tt):
        return pltpu.make_async_remote_copy(
            src_ref=src, dst_ref=dst, send_sem=ssem, recv_sem=rsem,
            device_id=(cc, tt), device_id_type=MESH,
        )

    loads = [
        pltpu.make_async_copy(src, dst, load_sem.at[n])
        for n, (src, dst) in enumerate([
            (pg_ref, pgt), (x_ref, xs), (nw_ref, nws), (a_ref, am), (q_ref, qs),
            (k_ref, kx.at[pl.ds(1024, ROWS), :]), (v_ref, vx.at[pl.ds(1024, ROWS), :]),
            (doc_ref, ids.at[:, pl.ds(1024, ROWS)]),
        ])
    ]

    def order_of(s):
        first_x = ((s + 1) // 2) % 2
        first_y = 2 + (s // 2) * ((s % 2) * 2 - 1)
        late = s - 4
        late_x = s % 2
        late_y = (1 - late // 2) * (1 + 2 * (s % 2))
        is_late = s // 4
        dx = first_x * (1 - is_late) + late_x * is_late
        dy = first_y * (1 - is_late) + late_y * is_late
        return dx * 4 + (y + dy) % 4

    def wload(s):
        cols = pl.ds(pl.multiple_of(order_of(s) * QCOLS, QCOLS), QCOLS)
        return pltpu.make_async_copy(w_ref.at[:, cols], ws.at[s], wload_sem.at[s])

    loads[0].start()
    loop(2, lambda s: wload(s).start())

    barrier = pltpu.get_barrier_semaphore()

    def greet_y(d):
        pl.semaphore_signal(
            barrier, inc=1, device_id=(c, xh * 4 + (y + d) % 4), device_id_type=MESH
        )

    def meet(sem, d):
        pl.semaphore_signal(sem, inc=1, device_id=((c + d) % CTX, t), device_id_type=MESH)
        pl.semaphore_signal(sem, inc=1, device_id=((c + CTX - d) % CTX, t), device_id_type=MESH)

    for d in (2, 1, 3):
        greet_y(d)
    pl.semaphore_signal(barrier, inc=1, device_id=(c, across), device_id_type=MESH)
    meet(barrier, 1)
    meet(barrier, 2)


    def rows_of(rc):
        return pl.ds(pl.multiple_of(rc * RC, RC), RC)

    def p_copy(s, rc):
        turn = (y + 1 + 2 * (s % 2)) % 4
        return remote(
            psend.at[s, rows_of(rc), :], precv.at[s, rows_of(rc), :],
            p_send.at[s, rc], p_recv.at[s, rc], c, xh * 4 + turn,
        )

    def a_copy(s, rc):
        turn = (y + 1 + 2 * s) % 4
        return remote(
            asend.at[s, rows_of(rc), :], arecv.at[s, rows_of(rc), :],
            a_send.at[s, rc], a_recv.at[s, rc], c, xh * 4 + turn,
        )

    def x_copy(rc):
        return remote(
            xsend.at[rows_of(rc), :], xrecv.at[rows_of(rc), :],
            x_send.at[rc], x_recv.at[rc], c, across,
        )

    def early(s):
        wload(s).wait()
        psend[s] = dot(pgs[...], ws[s]).astype(BF16)

    def late(s):
        wload(s + 4).wait()
        pacc[s] = dot(pgs[...], ws[s + 4])

    last = pl.ds((NRC - 1) * RC, RC)

    def x_part(m):
        src = (
            psend.at[1 - xh, last, :], psend.at[2 + xh, last, :], bsend.at[0], bsend.at[1]
        )[m]
        slot = (0, 1 + xh, 2 - xh, 3)[m]
        return remote(src, zrecv.at[slot], z_send.at[m], z_recv.at[slot], c, across)

    def x_part_wait(slot):
        remote(bsend.at[0], zrecv.at[slot], z_send.at[0], z_recv.at[slot], c, t).wait_recv()

    def s_copy(n):
        return remote(
            ssend.at[n], srecv.at[n], s_send.at[n], s_recv.at[n], c, xh * 4 + (y + 1 + 2 * n) % 4
        )

    def f_copy(n):
        return remote(
            fsend.at[n], frecv.at[n], f_send.at[n], f_recv.at[n], c, xh * 4 + (y + 1 + 2 * n) % 4
        )

    def message(k, n):
        return (
            lambda: p_copy(n, 0), lambda: p_copy(n, 1), lambda: p_copy(n, 2),
            lambda: p_copy(2 + n, 0), lambda: a_copy(n, 0), lambda: s_copy(n),
            lambda: p_copy(2 + n, 1), lambda: a_copy(n, 1),
            lambda: p_copy(2 + n, 2), lambda: a_copy(n, 2), lambda: f_copy(n),
        )[k]()

    def issue(k):
        for n in range(2):
            if k >= 4:
                message(k - 4, n).wait_send()
            message(k, n).start()

    def pass_on(rc):
        for n in range(2):
            p_copy(n, rc).wait_recv()
            asend[n, rows_of(rc), :] = (
                pacc[n, rows_of(rc), :] + precv[n, rows_of(rc), :].astype(F32)
            ).astype(BF16)

    def id_copy(d):
        return remote(
            doc_ref, ids.at[:, pl.ds((2 - d) * ROWS, ROWS)], id_send.at[d - 1], id_recv.at[d - 1],
            (c + d) % CTX, t,
        )

    def kv_copy(m, hop):
        own, window = ((k_ref, kx), (v_ref, vx))[m]
        near = window.at[pl.ds(512, ROWS), :]
        far = window.at[pl.ds(0, ROWS), :]
        return remote(
            near if hop else own, far if hop else near,
            halo_send.at[m, hop], halo_recv.at[m, hop], (c + 1) % CTX, t,
        )

    loads[0].wait()
    pgs[0:RC, :] = jnp.transpose(pgt[:, 0:RC], (1, 0))

    def first(s):
        wload(s).wait()
        psend[s, 0:RC, :] = dot(pgs[0:RC, :], ws[s]).astype(BF16)

    loop(2, first)
    pl.semaphore_wait(barrier, 4 + 4)

    issue(0)
    for copy in loads[1:]:
        copy.start()
    loop(6, lambda s: wload(s + 2).start())
    pgs[RC:ROWS, :] = jnp.transpose(pgt[:, RC:ROWS], (1, 0))

    def second(s):
        psend[s, RC:ROWS, :] = dot(pgs[RC:ROWS, :], ws[s]).astype(BF16)

    loop(2, second)
    x_part(0).start()
    kv_copy(0, 0).start()
    issue(1)
    id_copy(1).start()
    id_copy(2).start()
    kv_copy(1, 0).start()
    meet(known.at[0], 2)
    pl.semaphore_signal(known.at[3], inc=1, device_id=(c, across), device_id_type=MESH)

    for copy in loads[1:4]:
        copy.wait()
    sel_row = lax.broadcasted_iota(jnp.int32, (32, 3 * RANK), 0)
    sel_col = lax.broadcasted_iota(jnp.int32, (32, 3 * RANK), 1)
    wanted = jnp.where(sel_row < 16, sel_row + 8, jnp.where(sel_row < 24, sel_row - 16, -1))
    select = (wanted == sel_col).astype(BF16)
    maps = dot(select, am[...]) * nws[...].astype(F32).reshape(1, WIDTH)
    maps_hi = maps.astype(BF16)
    maps_lo = (maps - maps_hi.astype(F32)).astype(BF16)
    x_low = xs[...]
    part = dot(maps_hi, x_low) + dot(maps_lo, x_low)
    x_wide = x_low.astype(F32)
    square = x_wide * x_wide
    square_hi = square.astype(BF16)
    square_lo = (square - square_hi.astype(F32)).astype(BF16)
    ones = jnp.ones((RANK, WIDTH), BF16)
    squares = dot(ones, square_hi) + dot(ones, square_lo)
    for n in range(4):
        cols = slice(n * 128, (n + 1) * 128)
        tmine[n, 0:24, :] = part[0:24, cols]
        tmine[n, 24:32, :] = squares[:, cols]

    def t1_copy(d):
        dest = (y + d) % 4
        return remote(tmine.at[dest], trecv.at[y], t1_send.at[d], t1_recv.at[y], c, xh * 4 + dest)

    def t1_wait(d):
        src = (y + d) % 4
        remote(tmine.at[y], trecv.at[src], t1_send.at[d], t1_recv.at[src], c, t).wait_recv()
        t1_copy(d).wait_send()

    loop(3, lambda d: t1_copy(d + 1).start())

    loop(2, lambda s: early(s + 2))
    issue(2)
    loop(2, late)
    bsend[0] = pacc[1 - xh, last, :].astype(BF16)

    loop(3, lambda d: t1_wait(d + 1))
    tsum = tmine[y]
    for d in range(1, 4):
        tsum = tsum + trecv[(y + d) % 4]
    tx_send[...] = tsum
    t2 = remote(tx_send, tx_recv, t2_send, t2_recv, c, across)
    t2.start()
    loop(2, lambda s: late(s + 2))
    bsend[1] = pacc[3 - xh, last, :].astype(BF16)
    issue(3)
    kv_copy(0, 0).wait_recv()
    kv_copy(0, 1).start()
    x_part(1).start()
    x_part(2).start()
    pl.semaphore_wait(known.at[0], 2)
    meet(known.at[1], 4)
    pass_on(0)
    issue(4)
    x_part(3).start()

    t2.wait()
    tfull = tx_send[...] + tx_recv[...]
    rstd = lax.rsqrt(tfull[24:32, :] * (1.0 / MODEL_WIDTH) + 1e-06)
    lown[...] = (tfull * jnp.concatenate([rstd] * 4, axis=0)).astype(BF16)

    def own_cols(n):
        return pl.ds(pl.multiple_of(1024 + n * 128, 128), 128)

    lx[:, own_cols(y)] = lown[...]

    def t3_copy(d):
        return remote(
            lown, lx.at[:, own_cols(y)], t3_send.at[d], t3_recv.at[y], c, xh * 4 + (y + d) % 4
        )

    def t3_wait(d):
        src = (y + d) % 4
        remote(lown, lx.at[:, own_cols(src)], t3_send.at[d], t3_recv.at[src], c, t).wait_recv()
        t3_copy(d).wait_send()

    loop(3, lambda d: t3_copy(d + 1).start())
    for copy in loads[4:]:
        copy.wait()
    id_copy(1).wait()
    id_copy(2).wait()
    key_at = lax.broadcasted_iota(jnp.int32, (1, WINDOW), 1) + c * ROWS - LOOKBACK_SPAN
    key_ids = jnp.where(key_at < 0, -1, ids[...]).astype(F32)
    own_ids = jnp.broadcast_to(key_ids[:, 1024:1536], (128, ROWS))
    query_ids = jnp.transpose(own_ids, (1, 0))
    row_at = lax.broadcasted_iota(jnp.int32, (RC, 128), 0)
    col_at = lax.broadcasted_iota(jnp.int32, (RC, 128), 1)
    for b in range(NRC):
        for m in range(KSPAN // 128):
            start = (b + m) * 128
            spacing = 1024 - m * 128 + row_at - col_at
            allowed = query_ids[b * RC:(b + 1) * RC, :] == key_ids[:, start:start + 128]
            allowed = allowed & (spacing >= 0) & (spacing < LOOKBACK_SPAN)
            bias[b, :, m * 128:(m + 1) * 128] = jnp.where(allowed, 0.0, -1e30)

    def parts_of(i):
        rc, group = i // 2, i % 2
        k_rows = pl.ds(pl.multiple_of(rc * RC, RC), KSPAN)
        g_cols = pl.ds(pl.multiple_of(group * HEAD_SIZE, HEAD_SIZE), HEAD_SIZE)
        return rc, group, k_rows, g_cols

    def both_heads(ref, rc, group):
        return jnp.concatenate([
            ref[rows_of(rc), pl.ds(pl.multiple_of((2 * group + n) * HEAD_SIZE, HEAD_SIZE), HEAD_SIZE)]
            for n in range(2)
        ], axis=0)

    def softmax(i):
        rc, group, k_rows, g_cols = parts_of(i)
        scores = dot(both_heads(qs, rc, group), kx[k_rows, g_cols], NT) * (SCALE * LOG2E)
        scores = (scores.reshape(2, RC, KSPAN) + bias[rc][None]).reshape(2 * RC, KSPAN)
        highest = jnp.max(scores, axis=-1, keepdims=True)
        expons = jnp.exp2(scores - highest)
        total = jnp.sum(expons, axis=-1, keepdims=True)
        probs[i] = expons * (1.0 / total)

    def value_side(i):
        rc, group, k_rows, g_cols = parts_of(i)
        rv[i] = dot(lx[0:16, k_rows], probs[i].astype(BF16), NT)

    def finish(rc):
        rows = rows_of(rc)
        for n in range(2):
            p_copy(2 + n, rc).wait_recv()
            a_copy(n, rc).wait_recv()
        xsend[rows, :] = (
            pacc[3 - xh, rows, :] + arecv[1 - xh, rows, :].astype(F32)
            + precv[2 + xh, rows, :].astype(F32)
        ).astype(BF16)
        x_copy(rc).start()
        pacc[2 + xh, rows, :] = (
            pacc[2 + xh, rows, :] + arecv[xh, rows, :].astype(F32)
            + precv[3 - xh, rows, :].astype(F32)
        )

    def take(rc):
        rows = rows_of(rc)
        x_copy(rc).wait_recv()
        g[rows, :] = (pacc[2 + xh, rows, :] + xrecv[rows, :].astype(F32)).astype(BF16)

    def backward(i):
        rc, group, k_rows, g_cols = parts_of(i)
        grad = both_heads(g, rc, group)
        grad_probs = dot(grad, vx[k_rows, g_cols], NT)
        prob = probs[i]
        delta = jnp.sum(prob * grad_probs, axis=-1, keepdims=True)
        grad_scores = (prob * (grad_probs - delta)).astype(BF16)
        side_k = (dot(lx[0:16, k_rows], grad_scores, NT) * SCALE).astype(BF16)
        own = lx[16:32, pl.ds(pl.multiple_of(1024 + rc * RC, RC), RC)]
        none = jnp.zeros_like(own)
        own_both = jnp.concatenate([
            jnp.concatenate([own, none], axis=1), jnp.concatenate([none, own], axis=1)
        ], axis=0)
        side_q = (dot(own_both, grad_scores) * SCALE).astype(BF16)
        to_q = dot(side_q, kx[k_rows, g_cols])
        acc[2 * group] += to_q[0:8]
        acc[2 * group + 1] += to_q[16:24]
        acc[4 + group] += dot(side_k, both_heads(qs, rc, group))[0:8]
        acc[6 + group] += dot(rv[i].astype(BF16), grad)[8:16]

    acc[...] = jnp.zeros_like(acc)
    x_part_wait(0)
    far = psend[xh, last, :].astype(F32) + zrecv[0].astype(F32)
    ssend[0] = far[:, 0:256].astype(BF16)
    ssend[1] = far[:, 256:512].astype(BF16)
    issue(5)
    pass_on(1)
    issue(6)
    issue(7)

    loop(3, lambda d: t3_wait(d + 1))
    t4s = [
        remote(
            lx.at[pl.ds(0, 16), pl.ds(1024, ROWS)], lx.at[pl.ds(0, 16), pl.ds((1 - n) * ROWS, ROWS)],
            t4_send.at[n], t4_recv.at[n], (c + n + 1) % CTX, t,
        )
        for n in range(2)
    ]
    for copy in t4s:
        copy.start()

    kv_copy(1, 0).wait_recv()
    kv_copy(1, 1).start()
    kv_copy(0, 1).wait_recv()
    loop(2, softmax)

    pl.semaphore_wait(known.at[1], 2)
    meet(known.at[2], 8)
    loop(2, lambda i: softmax(i + 2))
    pass_on(2)
    issue(8)
    loop(2, lambda i: softmax(i + 4))
    issue(9)
    finish(0)
    loop(2, lambda i: softmax(i + 6))

    for slot in range(1, 4):
        x_part_wait(slot)
    zbuf[2 - xh] = psend[3 - xh, last, :].astype(F32) + zrecv[2 - xh].astype(F32)
    zbuf[1 + xh] = pacc[xh, last, :] + zrecv[1 + xh].astype(F32)
    zbuf[3] = pacc[2 + xh, last, :] + zrecv[3].astype(F32)
    for n in range(2):
        s_copy(n).wait_recv()
        passed = slice(n * 256, (n + 1) * 256)
        direct = slice((1 - n) * 256, (2 - n) * 256)
        fsend[n, :, passed] = (zbuf[1 + n, :, passed] + srecv[n].astype(F32)).astype(BF16)
        fsend[n, :, direct] = zbuf[1 + n, :, direct].astype(BF16)

    issue(10)
    for copy in t4s:
        copy.wait()
    loop(4, value_side)
    kv_copy(1, 1).wait_recv()
    take(0)
    finish(1)
    loop(2, backward)
    loop(4, lambda i: value_side(i + 4))
    finish(2)
    take(1)
    loop(2, lambda i: backward(i + 2))
    for n in range(2):
        f_copy(n).wait_recv()
    g[last, :] = (zbuf[3] + frecv[0].astype(F32) + frecv[1].astype(F32)).astype(BF16)
    loop(2, lambda i: backward(i + 6))
    take(2)
    loop(2, lambda i: backward(i + 4))
    pl.semaphore_wait(known.at[2], 2)
    pl.semaphore_wait(known.at[3], 1)

    def ar_copy(d):
        dest = (c + d) % CTX
        return remote(acc.at[dest // 4], ar.at[c], ar_send.at[d], ar_recv.at[c], dest, t)

    def ar_wait(d):
        src = (c + d) % CTX
        remote(acc.at[z], ar.at[src], ar_send.at[d], ar_recv.at[src], c, t).wait_recv()

    loop(CTX - 1, lambda i: ar_copy(16 + (i + 1) // 2 * (2 * (i % 2) - 1)).start())
    ar[c] = acc[z]
    for k in range(7, 11):
        for n in range(2):
            message(k, n).wait_send()
    for n in range(4):
        kv_copy(n // 2, n % 2).wait_send()
    for m in range(4):
        x_part(m).wait_send()
    loop(NRC - 1, lambda rc: x_copy(rc).wait_send())
    loop(CTX - 1, lambda d: ar_wait(d + 1))
    red[...] = jnp.sum(ar[...], axis=0)

    def spread(i):
        return 4 + (i + 1) // 2 * (2 * (i % 2) - 1)

    def fin_copy(d):
        return remote(
            red, fin.at[z], fin_send.at[d], fin_recv.at[z], ((z + d) % 8) * 4 + low, t
        )

    def fin_wait(d):
        src = (z + d) % 8
        remote(red, fin.at[src], fin_send.at[d], fin_recv.at[src], c, t).wait_recv()

    loop(7, lambda i: fin_copy(spread(i)).start())
    fin[z] = red[...]
    loop(CTX - 1, lambda d: ar_copy(d + 1).wait_send())
    loop(7, lambda d: fin_wait(d + 1))

    whole = fin[...]
    sq[...] = jnp.sum(whole * whole, axis=0)

    def sq_copy(d):
        return remote(sq, sqr.at[t], sq_send.at[d], sq_recv.at[t], c, (t + d) % 8)

    def sq_wait(d):
        src = (t + d) % 8
        remote(sq, sqr.at[src], sq_send.at[d], sq_recv.at[src], c, t).wait_recv()

    loop(7, lambda d: sq_copy(d + 1).start())
    sqr[t] = sq[...]
    loop(7, lambda d: fin_copy(d + 1).wait_send())
    loop(7, lambda d: sq_wait(d + 1))
    squared = jnp.sum(jnp.sum(jnp.sum(sqr[...], axis=0), axis=0, keepdims=True), axis=1, keepdims=True)
    factor = jnp.sqrt(
        float(RANK * (QUERY_HEADS + 2 * KEY_VALUE_HEADS) * HEAD_SIZE) / (squared + 1e-06)
    )
    out_ref[...] = fin[...] * factor
    loop(7, lambda d: sq_copy(d + 1).wait_send())


def split(sum_ref, oq_ref, ok_ref, ov_ref):
    for n in range(4):
        oq_ref[:, n * 128:(n + 1) * 128] = sum_ref[n]
    for n in range(2):
        ok_ref[:, n * 128:(n + 1) * 128] = sum_ref[4 + n]
        ov_ref[:, n * 128:(n + 1) * 128] = sum_ref[6 + n]


def per_device(x, nw, doc, q, k, v, w, pg, a):
    any_spec = pl.BlockSpec(memory_space=pl.ANY)
    vmem = pl.BlockSpec(memory_space=pltpu.VMEM)
    dma = pltpu.SemaphoreType.DMA
    summed = pl.pallas_call(
        kernel,
        out_shape=jax.ShapeDtypeStruct((8, RANK, HEAD_SIZE), F32),
        in_specs=[any_spec] * 9,
        out_specs=vmem,
        scratch_shapes=[
            pltpu.VMEM((WIDTH, ROWS), BF16),
            pltpu.VMEM((WIDTH,), BF16),
            pltpu.VMEM((1, WINDOW), jnp.int32),
            pltpu.VMEM((ROWS, QCOLS), BF16),
            pltpu.VMEM((WINDOW, KCOLS), BF16),
            pltpu.VMEM((WINDOW, KCOLS), BF16),
            pltpu.VMEM((8, WIDTH, QCOLS), BF16),
            pltpu.VMEM((WIDTH, ROWS), BF16),
            pltpu.VMEM((ROWS, WIDTH), BF16),
            pltpu.VMEM((3 * RANK, WIDTH), BF16),
            pltpu.VMEM((4, ROWS, QCOLS), BF16),
            pltpu.VMEM((4, ROWS, QCOLS), F32),
            pltpu.VMEM((4, ROWS, QCOLS), BF16),
            pltpu.VMEM((2, ROWS, QCOLS), BF16),
            pltpu.VMEM((2, ROWS, QCOLS), BF16),
            pltpu.VMEM((ROWS, QCOLS), BF16),
            pltpu.VMEM((ROWS, QCOLS), BF16),
            pltpu.VMEM((2, RC, QCOLS), BF16),
            pltpu.VMEM((4, RC, QCOLS), BF16),
            pltpu.VMEM((4, RC, QCOLS), F32),
            pltpu.VMEM((2, RC, QCOLS // 2), BF16),
            pltpu.VMEM((2, RC, QCOLS // 2), BF16),
            pltpu.VMEM((2, RC, QCOLS), BF16),
            pltpu.VMEM((2, RC, QCOLS), BF16),
            pltpu.VMEM((4, 32, 128), F32),
            pltpu.VMEM((4, 32, 128), F32),
            pltpu.VMEM((32, 128), F32),
            pltpu.VMEM((32, 128), F32),
            pltpu.VMEM((32, 128), BF16),
            pltpu.VMEM((32, WINDOW), BF16),
            pltpu.VMEM((NRC, RC, KSPAN), F32),
            pltpu.VMEM((8, 2 * RC, KSPAN), F32),
            pltpu.VMEM((8, 16, 2 * RC), F32),
            pltpu.VMEM((ROWS, QCOLS), BF16),
            pltpu.VMEM((8, RANK, 128), F32),
            pltpu.VMEM((CTX, RANK, 128), F32),
            pltpu.VMEM((RANK, 128), F32),
            pltpu.VMEM((8, RANK, 128), F32),
            pltpu.VMEM((RANK, 128), F32),
            pltpu.VMEM((8, RANK, 128), F32),
            dma((8,)), dma((8,)), dma((2, 2)), dma((2, 2)), dma((2,)), dma((2,)),
            pltpu.SemaphoreType.REGULAR((4,)),
            dma((4,)), dma((4,)), dma((2,)), dma((2,)), dma((2,)), dma((2,)),
            dma((4, NRC)), dma((4, NRC)), dma((2, NRC)), dma((2, NRC)), dma((NRC,)), dma((NRC,)),
            dma((4,)), dma((4,)), dma, dma, dma((4,)), dma((4,)), dma((2,)), dma((2,)),
            dma((CTX,)), dma((CTX,)), dma((8,)), dma((8,)), dma((8,)), dma((8,)),
        ],
        compiler_params=pltpu.CompilerParams(
            collective_id=0, has_side_effects=True, vmem_limit_bytes=60 * 1024 * 1024
        ),
        cost_estimate=pl.CostEstimate(
            flops=8_000_000_000, bytes_accessed=10_000_000, transcendentals=3_000_000
        ),
    )(x.T, nw, doc.reshape(1, ROWS), q, k, v, w.T, pg.T, a.T)
    return pl.pallas_call(
        split,
        out_shape=(
            jax.ShapeDtypeStruct((RANK, QCOLS), F32),
            jax.ShapeDtypeStruct((RANK, KCOLS), F32),
            jax.ShapeDtypeStruct((RANK, KCOLS), F32),
        ),
        in_specs=[vmem],
        out_specs=(vmem, vmem, vmem),
    )(summed)


def solution(mesh):
    placed = (
        P("ctx", "tp"),
        P("tp"),
        P("ctx"),
        P("ctx", "tp"),
        P("ctx", "tp"),
        P("ctx", "tp"),
        P(None, "tp"),
        P("ctx", "tp"),
        P("tp", None),
    )
    return jax.shard_map(
        per_device,
        mesh=mesh,
        in_specs=placed,
        out_specs=(P(None, "tp"), P(None, "tp"), P(None, "tp")),
        check_vma=False,
    )
```
